32 devices in a mesh: tm: 8 (over z, y), fsdp: 4 (over x, core).
Axes of the slice: x: 2, y: 2, z: 4, core: 2. Of those that a mesh axis runs over, the one named last changes fastest.
Arguments:
- queries: bfloat16 [32, 128, 12, 128], P('tm', 'fsdp'), may hold values from -5 to 5
- key_states: bfloat16 [32, 128, 12, 128], P('tm', 'fsdp'), may hold values from -5 to 5
- value_states: bfloat16 [32, 128, 12, 128], P('tm', 'fsdp'), may hold values from -6 to 6
- out_grad: bfloat16 [32, 128, 3072], P('tm', 'fsdp'), may hold values from -6 to 6
- out_proj: bfloat16 [1536, 3072], P('fsdp'), may hold values from -0.109375 to 0.109375
Outputs:
- query_grad: bfloat16 [32, 128, 12, 128], P('tm', 'fsdp')
- key_grad: bfloat16 [32, 128, 12, 128], P('tm', 'fsdp')
- value_grad: bfloat16 [32, 128, 12, 128], P('tm', 'fsdp')
The draws below stay inside these ranges and needn't reach their ends.
All inputs are finite; a program needn't handle non-finite values.
Results may differ from the reference program's by a relative error of at most 0.03.
Values may be sent and summed in bfloat16 or wider, within the bound.
No kernel may reach another device: no remote copies, remote signals or barrier semaphores. Data moves between devices by JAX's collectives and lax.ppermute only.
A program may use at most 64 MiB of HBM per device.

```python
import math
import jax
import jax.numpy as jnp
from jax import lax

D = 3072
HEADS = 12
HEAD = 128
INNER = 1536
FRAMES = 32
POSITIONS = 128


def draw_queries(key, part):
    own = jax.random.fold_in(key, 1)
    shape = (FRAMES, POSITIONS, HEADS, HEAD)
    values = jnp.clip(jax.random.normal(own, shape, jnp.float32), -4.0, 4.0)
    return values.astype(jnp.bfloat16)


def draw_key_states(key, part):
    own = jax.random.fold_in(key, 2)
    shape = (FRAMES, POSITIONS, HEADS, HEAD)
    values = jnp.clip(jax.random.normal(own, shape, jnp.float32), -4.0, 4.0)
    return values.astype(jnp.bfloat16)


def steps_of(rng, shape, pieces, low, top_value):
    def one(position, shards_of):
        draws = jax.random.uniform(jax.random.fold_in(jax.random.fold_in(rng, 6), position), (shards_of,), jnp.float32, low / len(pieces), top_value / len(pieces))
        return jnp.repeat(jnp.exp(draws), shape[position] // shards_of).reshape((-1,) + (1,) * (len(shape) - position - 1))

    level = one(*pieces[0])
    for cut in pieces[1:]:
        level = level * one(*cut)
    return level


def bell_draw(stream_key, dims, scale, bound, cuts=(), dtype=jnp.bfloat16):
    gain = steps_of(stream_key, dims, cuts, -0.22, 0.18) if cuts else 1.0
    result = jax.random.normal(stream_key, dims, jnp.float32) * scale * gain
    return jnp.minimum(jnp.maximum(result, -bound), bound).astype(dtype)


def setup_inputs(seed: int = 0) -> dict:
    seeds = jax.random.split(jax.random.key(seed), 6)
    return {
        "queries": draw_queries(jax.random.fold_in(seeds[5], 71), 0),
        "key_states": draw_key_states(jax.random.fold_in(seeds[5], 71), 0),
        "value_states": bell_draw(seeds[2], (FRAMES, POSITIONS, HEADS, HEAD), 1.0, 6.0, ((0, 8), (1, 4))),
        "out_grad": bell_draw(seeds[3], (FRAMES, POSITIONS, D), 1.0, 6.0, ((0, 8), (1, 4))),
        "out_proj": bell_draw(seeds[4], (INNER, D), D ** -0.5, 0.109375, ((0, 4),)),
    }


def attend_back(query_block, key_block, value_block, grad_block):
    score_scale = HEAD ** -0.5
    query_wide = query_block.astype(jnp.float32)
    key_wide = key_block.astype(jnp.float32)
    value_wide = value_block.astype(jnp.float32)
    grad_wide = grad_block.astype(jnp.float32)
    scores = jnp.einsum("fphd,gphd->phfg", query_wide, key_wide) * score_scale
    peak = jnp.max(scores, axis=-1, keepdims=True)
    expo = jnp.exp(scores - peak)
    probs = expo / jnp.sum(expo, axis=-1, keepdims=True)
    probs_b = probs.astype(jnp.bfloat16)
    probs_wide = probs_b.astype(jnp.float32)
    attn_out = jnp.einsum("phfg,gphd->fphd", probs_wide, value_wide)
    row_delta = jnp.einsum("fphd,fphd->phf", grad_wide, attn_out)
    dprobs = jnp.einsum("fphd,gphd->phfg", grad_wide, value_wide)
    dscores = (probs * (dprobs - row_delta[..., None])).astype(jnp.bfloat16).astype(jnp.float32)
    query_grad = (jnp.einsum("phfg,gphd->fphd", dscores, key_wide) * score_scale).astype(jnp.bfloat16)
    key_grad = (jnp.einsum("phfg,fphd->gphd", dscores, query_wide) * score_scale).astype(jnp.bfloat16)
    value_grad = jnp.einsum("phfg,fphd->gphd", probs_wide, grad_wide).astype(jnp.bfloat16)
    return query_grad, key_grad, value_grad


def reference(queries, key_states, value_states, out_grad, out_proj):
    flat = out_grad.reshape(FRAMES * POSITIONS, D)
    grad_attn = jnp.dot(flat, out_proj.T, preferred_element_type=jnp.float32).astype(jnp.bfloat16)
    grad_attn = grad_attn.reshape(FRAMES, POSITIONS, HEADS, HEAD)
    block = math.gcd(POSITIONS, 16)
    count = POSITIONS // block

    def split_blocks(array):
        return jnp.transpose(array.reshape(FRAMES, count, block, HEADS, HEAD), (1, 0, 2, 3, 4))

    def join_blocks(array):
        return jnp.transpose(array, (1, 0, 2, 3, 4)).reshape(FRAMES, POSITIONS, HEADS, HEAD)

    def one_block(items):
        return attend_back(items[0], items[1], items[2], items[3])

    outputs = lax.map(one_block, (split_blocks(queries), split_blocks(key_states), split_blocks(value_states), split_blocks(grad_attn)))
    return join_blocks(outputs[0]), join_blocks(outputs[1]), join_blocks(outputs[2])
```

```python
import functools

import jax
import jax.numpy as jnp
from jax import lax
from jax.experimental import pallas as pl
from jax.experimental.pallas import tpu as pltpu
from jax.sharding import PartitionSpec as P

ANY = pl.BlockSpec(memory_space=pl.ANY)
VMEM_LIMIT = 48 * 1024 * 1024
GROUPS = 4


def attend_back(query_block, key_block, value_block, grad_block):
    score_scale = query_block.shape[-1] ** (-0.5)
    scores = (
        jnp.einsum("fphd,gphd->phfg", query_block, key_block, preferred_element_type=jnp.float32)
        * score_scale
    )
    peak = jnp.max(scores, axis=-1, keepdims=True)
    expo = jnp.exp(scores - peak)
    probs = expo / jnp.sum(expo, axis=-1, keepdims=True)
    probs_b = probs.astype(jnp.bfloat16)
    attn_out = jnp.einsum(
        "phfg,gphd->fphd", probs_b, value_block, preferred_element_type=jnp.float32
    )
    row_delta = jnp.einsum("fphd,fphd->phf", grad_block.astype(jnp.float32), attn_out)
    dprobs = jnp.einsum(
        "fphd,gphd->phfg", grad_block, value_block, preferred_element_type=jnp.float32
    )
    dscores = (probs * (dprobs - row_delta[..., None])).astype(jnp.bfloat16)
    query_grad = (
        jnp.einsum("phfg,gphd->fphd", dscores, key_block, preferred_element_type=jnp.float32)
        * score_scale
    ).astype(jnp.bfloat16)
    key_grad = (
        jnp.einsum("phfg,fphd->gphd", dscores, query_block, preferred_element_type=jnp.float32)
        * score_scale
    ).astype(jnp.bfloat16)
    value_grad = jnp.einsum(
        "phfg,fphd->gphd", probs_b, grad_block, preferred_element_type=jnp.float32
    ).astype(jnp.bfloat16)
    return (query_grad, key_grad, value_grad)


def body_any(queries, key_states, value_states, out_grad, out_proj):
    frames_dev, pos_dev, heads, head_size = queries.shape
    flat = out_grad.reshape(frames_dev * pos_dev, out_grad.shape[-1])
    grad_attn = (
        lax.dot_general(
            flat,
            lax.all_gather(out_proj, "fsdp", axis=0, tiled=True),
            (((1,), (1,)), ((), ())),
            preferred_element_type=jnp.float32,
        )
        .astype(jnp.bfloat16)
        .reshape(frames_dev, pos_dev, heads, head_size)
    )
    there = functools.partial(
        lax.all_to_all, axis_name="tm", split_axis=1, concat_axis=0, tiled=True
    )
    back = functools.partial(
        lax.all_to_all, axis_name="tm", split_axis=0, concat_axis=1, tiled=True
    )
    grads = attend_back(there(queries), there(key_states), there(value_states), there(grad_attn))
    return tuple(back(g) for g in grads)


def group_of(tm):
    return 2 * lax.rem(tm, 2) + lax.rem(tm // 2, 2)


def part_of(tm):
    return tm // GROUPS


def copy_all(copies):
    for copy in copies:
        copy.start()
    for copy in copies:
        copy.wait()


def pack_kernel(n_tm, q_ref, k_ref, v_ref, *refs):
    outs, sems = refs[:n_tm], refs[n_tm]
    me = lax.axis_index("tm")
    _, _, g_heads, p_rows, _ = outs[0].shape
    copies = []
    for k in range(n_tm - 1, -1, -1):
        there = me ^ k
        heads = pl.ds(group_of(there) * g_heads, g_heads)
        rows = pl.ds(pl.multiple_of(part_of(there) * p_rows, p_rows), p_rows)
        for a, ref in enumerate((q_ref, k_ref, v_ref)):
            copies.append(
                pltpu.make_async_copy(ref.at[:, heads, rows], outs[k].at[a], sems.at[3 * k + a])
            )
    copy_all(copies)


def pack(q, k, v, n_tm, p_rows):
    frames_dev, heads, _, head_size = q.shape
    shape = (3, frames_dev, heads // GROUPS, p_rows, head_size)
    return pl.pallas_call(
        functools.partial(pack_kernel, n_tm),
        out_shape=[jax.ShapeDtypeStruct(shape, q.dtype)] * n_tm,
        in_specs=[ANY] * 3,
        out_specs=[ANY] * n_tm,
        scratch_shapes=[pltpu.SemaphoreType.DMA((3 * n_tm,))],
        compiler_params=pltpu.CompilerParams(vmem_limit_bytes=VMEM_LIMIT),
        name="pack",
    )(q, k, v)


def unpack_kernel(n_tm, *refs):
    slots, outs, sems = refs[:n_tm], refs[n_tm : n_tm + 3], refs[n_tm + 3]
    me = lax.axis_index("tm")
    _, _, g_heads, p_rows, _ = slots[0].shape
    copies = []
    for k in range(n_tm):
        there = me ^ k
        heads = pl.ds(group_of(there) * g_heads, g_heads)
        rows = pl.ds(pl.multiple_of(part_of(there) * p_rows, p_rows), p_rows)
        for a, ref in enumerate(outs):
            copies.append(
                pltpu.make_async_copy(slots[k].at[a], ref.at[:, heads, rows], sems.at[3 * k + a])
            )
    copy_all(copies)


def unpack(slots, pos_dev):
    n_tm = len(slots)
    _, frames_dev, g_heads, _, head_size = slots[0].shape
    shape = (frames_dev, g_heads * GROUPS, pos_dev, head_size)
    return pl.pallas_call(
        functools.partial(unpack_kernel, n_tm),
        out_shape=[jax.ShapeDtypeStruct(shape, slots[0].dtype)] * 3,
        in_specs=[ANY] * n_tm,
        out_specs=[ANY] * 3,
        scratch_shapes=[pltpu.SemaphoreType.DMA((3 * n_tm,))],
        compiler_params=pltpu.CompilerParams(vmem_limit_bytes=VMEM_LIMIT),
        name="unpack",
    )(*slots)


def project_kernel(n_tm, own_ref, other_ref, w_own_ref, w_other_ref, *refs):
    outs, res, sems = refs[:n_tm], refs[n_tm], refs[n_tm + 1]
    me = lax.axis_index("tm")
    fs = lax.axis_index("fsdp")
    half, core = fs // 2, lax.rem(fs, 2)
    _, _, g_heads, frames_dev, pos_dev, head_size = res.shape
    p_rows = outs[0].shape[2]
    width = own_ref.shape[-1]
    for s, src in enumerate((own_ref, other_ref)):
        rows = src[...].reshape(frames_dev * pos_dev, width)
        for w, w_ref in enumerate((w_own_ref, w_other_ref)):
            out = lax.dot_general(
                rows,
                w_ref[...],
                (((1,), (1,)), ((), ())),
                preferred_element_type=jnp.float32,
            ).astype(jnp.bfloat16)
            for h in range(g_heads):
                res[s, core ^ w, h] = out[:, h * head_size : (h + 1) * head_size].reshape(
                    frames_dev, pos_dev, head_size
                )
    y, z = lax.rem(me, 2), me // 2
    copies = []
    for r in range(n_tm):
        kz, kx = r // 2, r % 2
        there_z, there_x = z ^ kz, y ^ kx
        rows = pl.ds(pl.multiple_of((there_z // 2) * p_rows, p_rows), p_rows)
        copies.append(
            pltpu.make_async_copy(
                res.at[half ^ there_x, lax.rem(there_z, 2), :, :, rows],
                outs[r],
                sems.at[r],
            )
        )
    copy_all(copies)


def project(own, other, w_own, w_other, n_tm, p_rows, head_size):
    frames_dev, pos_dev, width = own.shape
    g_heads = w_own.shape[0] // head_size
    shape = (g_heads, frames_dev, p_rows, head_size)
    rows = 2 * frames_dev * pos_dev
    return pl.pallas_call(
        functools.partial(project_kernel, n_tm),
        out_shape=[jax.ShapeDtypeStruct(shape, own.dtype)] * n_tm,
        in_specs=[pl.BlockSpec(memory_space=pltpu.VMEM)] * 4,
        out_specs=[ANY] * n_tm,
        scratch_shapes=[
            pltpu.VMEM((2, 2, g_heads, frames_dev, pos_dev, head_size), jnp.bfloat16),
            pltpu.SemaphoreType.DMA((n_tm,)),
        ],
        compiler_params=pltpu.CompilerParams(vmem_limit_bytes=VMEM_LIMIT),
        cost_estimate=pl.CostEstimate(
            flops=4 * rows * w_own.shape[0] * width,
            bytes_accessed=2 * width * (rows + 2 * w_own.shape[0]),
            transcendentals=0,
        ),
        name="project",
    )(own, other, w_own, w_other)


def attend_kernel(n_tm, *refs):
    qkv, gin = refs[:n_tm], refs[n_tm : 2 * n_tm]
    outs = refs[2 * n_tm : 3 * n_tm]
    qkv_s, g_s, wide, back, qkv_sem, g_sem = refs[3 * n_tm :]
    me = lax.axis_index("tm")
    half = lax.axis_index("fsdp") // 2
    _, _, frames_dev, g_heads, p_rows, head_size = qkv_s.shape
    frames = n_tm * frames_dev
    scale = head_size ** (-0.5)
    twist = half ^ lax.rem(me, 2)
    copies = []
    for k in range(n_tm):
        copies.append(pltpu.make_async_copy(qkv[k], qkv_s.at[k], qkv_sem.at[k]))
    for r in range(n_tm):
        slot = 2 * (r // 2) + (twist ^ (r % 2))
        copies.append(pltpu.make_async_copy(gin[r], g_s.at[slot], g_sem.at[r]))
    copy_all(copies)

    per = max(1, 128 // frames)
    block = per * frames
    row = lax.broadcasted_iota(jnp.int32, (block, block), 0) // frames
    col = lax.broadcasted_iota(jnp.int32, (block, block), 1) // frames
    same = row == col
    nt = (((1,), (1,)), ((), ()))
    nn = (((1,), (0,)), ((), ()))
    tn = (((0,), (0,)), ((), ()))
    dot = functools.partial(lax.dot_general, preferred_element_type=jnp.float32)

    for h in range(g_heads):
        for a in range(3):
            wide[a] = (
                qkv_s[:, a, :, h].reshape(frames * p_rows, head_size).astype(jnp.float32)
            )
        wide[3] = g_s[:, h].reshape(frames * p_rows, head_size).astype(jnp.float32)
        for b in range(p_rows // per):

            def rows_of(a):
                return jnp.concatenate(
                    [wide[a, pl.ds(b * per + j, frames, stride=p_rows), :] for j in range(per)],
                    axis=0,
                ).astype(jnp.bfloat16)

            q, k, v, g = rows_of(0), rows_of(1), rows_of(2), rows_of(3)
            scores = jnp.where(same, dot(q, k, nt) * scale, -jnp.inf)
            expo = jnp.exp(scores - jnp.max(scores, axis=-1, keepdims=True))
            probs = expo / jnp.sum(expo, axis=-1, keepdims=True)
            probs_b = probs.astype(jnp.bfloat16)
            dprobs = dot(g, v, nt)
            row_delta = jnp.sum(probs_b.astype(jnp.float32) * dprobs, axis=-1, keepdims=True)
            dscores = (probs * (dprobs - row_delta)).astype(jnp.bfloat16)
            grads = (
                dot(dscores, k, nn) * scale,
                dot(dscores, q, tn) * scale,
                dot(probs_b, g, tn),
            )
            for a, grad in enumerate(grads):
                for j in range(per):
                    back[a, pl.ds(b * per + j, frames, stride=p_rows), :] = grad[
                        j * frames : (j + 1) * frames
                    ]
        for a in range(3):
            done = back[a].astype(jnp.bfloat16).reshape(n_tm, frames_dev, p_rows, head_size)
            for k in range(n_tm):
                outs[k][a, :, h] = done[k]


def attend(qkv, gin):
    n_tm = len(qkv)
    shape = qkv[0].shape
    _, frames_dev, g_heads, p_rows, head_size = shape
    frames = n_tm * frames_dev
    return pl.pallas_call(
        functools.partial(attend_kernel, n_tm),
        out_shape=[jax.ShapeDtypeStruct(shape, qkv[0].dtype)] * n_tm,
        in_specs=[ANY] * (2 * n_tm),
        out_specs=[pl.BlockSpec(memory_space=pltpu.VMEM)] * n_tm,
        scratch_shapes=[
            pltpu.VMEM((n_tm,) + shape, jnp.bfloat16),
            pltpu.VMEM((n_tm, g_heads, frames_dev, p_rows, head_size), jnp.bfloat16),
            pltpu.VMEM((4, frames * p_rows, head_size), jnp.float32),
            pltpu.VMEM((3, frames * p_rows, head_size), jnp.float32),
            pltpu.SemaphoreType.DMA((n_tm,)),
            pltpu.SemaphoreType.DMA((n_tm,)),
        ],
        compiler_params=pltpu.CompilerParams(vmem_limit_bytes=VMEM_LIMIT),
        name="attend",
    )(*qkv, *gin)


def body_permutes(n_tm, n_fsdp, queries, key_states, value_states, out_grad, out_proj):
    frames_dev, pos_dev, heads, head_size = queries.shape
    p_rows = pos_dev * GROUPS // n_tm

    def swap(x, bit):
        return lax.ppermute(x, "fsdp", [(i, i ^ bit) for i in range(n_fsdp)])

    def over_tm(messages):
        return [messages[0]] + [
            lax.ppermute(messages[k], "tm", [(i, i ^ k) for i in range(n_tm)])
            for k in range(1, n_tm)
        ]

    def round_of(message, r):
        kz, kx = r // 2, r % 2
        pairs = []
        for tm in range(n_tm):
            for fs in range(n_fsdp):
                z, y, x, core = tm // 2, tm % 2, fs // 2, fs % 2
                there = (2 * (z ^ kz) + x) * n_fsdp + 2 * (y ^ kx) + core
                pairs.append((tm * n_fsdp + fs, there))
        return lax.ppermute(message, ("tm", "fsdp"), pairs)

    other = swap(out_grad, 2)
    w_other = swap(out_proj, 1)
    heads_out = lambda x: jnp.transpose(x, (0, 2, 1, 3))
    qkv = over_tm(
        pack(heads_out(queries), heads_out(key_states), heads_out(value_states), n_tm, p_rows)
    )
    messages = project(out_grad, other, out_proj, w_other, n_tm, p_rows, head_size)
    gin = [round_of(m, r) for r, m in enumerate(messages)]
    grads = over_tm(attend(qkv, gin))
    return tuple(heads_out(g) for g in unpack(grads, pos_dev))


def solution(mesh):
    n_tm, n_fsdp = mesh.shape["tm"], mesh.shape["fsdp"]

    def body(queries, key_states, value_states, out_grad, out_proj):
        _, pos_dev, heads, head_size = queries.shape
        fits = (
            n_tm == 2 * GROUPS
            and n_fsdp == GROUPS
            and heads % GROUPS == 0
            and out_proj.shape[0] * GROUPS == heads * head_size
            and pos_dev % 32 == 0
            and head_size == 128
        )
        if fits:
            return body_permutes(
                n_tm, n_fsdp, queries, key_states, value_states, out_grad, out_proj
            )
        return body_any(queries, key_states, value_states, out_grad, out_proj)

    return jax.shard_map(
        body,
        mesh=mesh,
        in_specs=(
            P("tm", "fsdp", None, None),
            P("tm", "fsdp", None, None),
            P("tm", "fsdp", None, None),
            P("tm", "fsdp", None),
            P("fsdp", None),
        ),
        out_specs=(
            P("tm", "fsdp", None, None),
            P("tm", "fsdp", None, None),
            P("tm", "fsdp", None, None),
        ),
        check_vma=False,
    )
```

```python
import functools

import jax
import jax.numpy as jnp
from jax import lax
from jax.experimental import pallas as pl
from jax.experimental.pallas import tpu as pltpu
from jax.sharding import PartitionSpec as P

ANY = pl.BlockSpec(memory_space=pl.ANY)
HBM = pl.BlockSpec(memory_space=pltpu.HBM)
VMEM = pl.BlockSpec(memory_space=pltpu.VMEM)
MIB = 1024 * 1024
SLOTS = (7, 4, 6, 5, 3, 2, 1, 0)
ROUNDS = (0, 1, 2, 3, 4, 5, 6, 7)
GROUPS = 4


NT = (((1,), (1,)), ((), ()))
dot = functools.partial(lax.dot_general, preferred_element_type=jnp.float32)


def blocks_dot(a, b, over_a, over_b):
    return dot(a, b, (((over_a,), (over_b,)), ((0,), (0,))))


def attend_back(query_block, key_block, value_block, grad_block):
    score_scale = query_block.shape[-1] ** (-0.5)
    scores = (
        jnp.einsum("fphd,gphd->phfg", query_block, key_block, preferred_element_type=jnp.float32)
        * score_scale
    )
    peak = jnp.max(scores, axis=-1, keepdims=True)
    expo = jnp.exp(scores - peak)
    probs = expo / jnp.sum(expo, axis=-1, keepdims=True)
    probs_b = probs.astype(jnp.bfloat16)
    attn_out = jnp.einsum(
        "phfg,gphd->fphd", probs_b, value_block, preferred_element_type=jnp.float32
    )
    row_delta = jnp.einsum("fphd,fphd->phf", grad_block.astype(jnp.float32), attn_out)
    dprobs = jnp.einsum(
        "fphd,gphd->phfg", grad_block, value_block, preferred_element_type=jnp.float32
    )
    dscores = (probs * (dprobs - row_delta[..., None])).astype(jnp.bfloat16)
    query_grad = (
        jnp.einsum("phfg,gphd->fphd", dscores, key_block, preferred_element_type=jnp.float32)
        * score_scale
    ).astype(jnp.bfloat16)
    key_grad = (
        jnp.einsum("phfg,fphd->gphd", dscores, query_block, preferred_element_type=jnp.float32)
        * score_scale
    ).astype(jnp.bfloat16)
    value_grad = jnp.einsum(
        "phfg,fphd->gphd", probs_b, grad_block, preferred_element_type=jnp.float32
    ).astype(jnp.bfloat16)
    return (query_grad, key_grad, value_grad)


def body_any(queries, key_states, value_states, out_grad, out_proj):
    frames_dev, pos_dev, heads, head_size = queries.shape
    flat = out_grad.reshape(frames_dev * pos_dev, out_grad.shape[-1])
    grad_attn = (
        lax.dot_general(
            flat,
            lax.all_gather(out_proj, "fsdp", axis=0, tiled=True),
            (((1,), (1,)), ((), ())),
            preferred_element_type=jnp.float32,
        )
        .astype(jnp.bfloat16)
        .reshape(frames_dev, pos_dev, heads, head_size)
    )
    there = functools.partial(
        lax.all_to_all, axis_name="tm", split_axis=1, concat_axis=0, tiled=True
    )
    back = functools.partial(
        lax.all_to_all, axis_name="tm", split_axis=0, concat_axis=1, tiled=True
    )
    grads = attend_back(there(queries), there(key_states), there(value_states), there(grad_attn))
    return tuple(back(g) for g in grads)


def group_of(tm):
    return 2 * (tm % 2) + tm // 2 % 2


def part_of(tm):
    return tm // GROUPS


def copy_all(copies):
    for copy in copies:
        copy.start()
    for copy in copies:
        copy.wait()


def pack_kernel(n_tm, q_ref, k_ref, v_ref, out, sems):
    _, _, _, g_heads, p_rows, _ = out.shape
    copies = []
    for i in range(n_tm):
        heads = slice(group_of(i) * g_heads, (group_of(i) + 1) * g_heads)
        rows = slice(part_of(i) * p_rows, (part_of(i) + 1) * p_rows)
        for a, ref in enumerate((q_ref, k_ref, v_ref)):
            copies.append(
                pltpu.make_async_copy(ref.at[:, heads, rows], out.at[i, a], sems.at[3 * i + a])
            )
    copy_all(copies)


def pack(q, k, v, n_tm, p_rows):
    frames_dev, heads, _, head_size = q.shape
    shape = (n_tm, 3, frames_dev, heads // GROUPS, p_rows, head_size)
    return pl.pallas_call(
        functools.partial(pack_kernel, n_tm),
        out_shape=jax.ShapeDtypeStruct(shape, q.dtype),
        in_specs=[HBM] * 3,
        out_specs=VMEM,
        scratch_shapes=[pltpu.SemaphoreType.DMA((3 * n_tm,))],
        compiler_params=pltpu.CompilerParams(vmem_limit_bytes=4 * MIB),
        name="pack",
    )(*(pltpu.with_memory_space_constraint(x, pltpu.HBM) for x in (q, k, v)))


def unpack_kernel(slots, *refs):
    n_tm = len(slots)
    grads, outs, sems = refs[:n_tm], refs[n_tm : n_tm + 3], refs[n_tm + 3]
    me = lax.axis_index("tm")
    _, _, g_heads, p_rows, _ = grads[0].shape
    copies = []
    for j, k in enumerate(slots):
        there = me ^ k
        heads = pl.ds(group_of(there) * g_heads, g_heads)
        rows = pl.ds(pl.multiple_of(part_of(there) * p_rows, p_rows), p_rows)
        for a, ref in enumerate(outs):
            copies.append(
                pltpu.make_async_copy(grads[j].at[a], ref.at[:, heads, rows], sems.at[3 * j + a])
            )
    copy_all(copies)


def unpack(grads, slots, pos_dev):
    n_tm = len(grads)
    _, frames_dev, g_heads, _, head_size = grads[0].shape
    shape = (frames_dev, g_heads * GROUPS, pos_dev, head_size)
    return pl.pallas_call(
        functools.partial(unpack_kernel, slots),
        out_shape=[jax.ShapeDtypeStruct(shape, grads[0].dtype)] * 3,
        in_specs=[ANY] * n_tm,
        out_specs=[HBM] * 3,
        scratch_shapes=[pltpu.SemaphoreType.DMA((3 * n_tm,))],
        compiler_params=pltpu.CompilerParams(vmem_limit_bytes=1 * MIB),
        name="unpack",
    )(*grads)


def project_kernel(n_tm, own_ref, other_ref, w_own_ref, w_other_ref, *refs):
    outs = refs[:n_tm]
    rows_ref, w_ref, res, row_sems, w_sems, out_sems = refs[n_tm:]
    me, fs = lax.axis_index("tm"), lax.axis_index("fsdp")
    half, core = fs // 2, lax.rem(fs, 2)
    _, _, g_heads, frames_dev, pos_dev, head_size = res.shape
    row_copies = [
        pltpu.make_async_copy(ref, rows_ref.at[i], row_sems.at[i])
        for i, ref in enumerate((own_ref, other_ref))
    ]
    w_copies = [
        pltpu.make_async_copy(ref, w_ref.at[i], w_sems.at[i])
        for i, ref in enumerate((w_own_ref, w_other_ref))
    ]
    for copy in (w_copies[0], *row_copies, w_copies[1]):
        copy.start()
    for copy in row_copies:
        copy.wait()
    rows = rows_ref[...].reshape(2 * frames_dev * pos_dev, rows_ref.shape[-1])
    for w in range(2):
        w_copies[w].wait()
        out = dot(rows, w_ref[w], NT).astype(jnp.bfloat16)
        for h in range(g_heads):
            res[core ^ w, :, h] = out[:, h * head_size : (h + 1) * head_size].reshape(
                2, frames_dev, pos_dev, head_size
            )
    p_rows = outs[0].shape[2]
    y, z = lax.rem(me, 2), me // 2
    copies = []
    for j, r in enumerate(ROUNDS):
        there_z, there_x = z ^ (r // 2), y ^ (r % 2)
        part = pl.ds(pl.multiple_of((there_z // 2) * p_rows, p_rows), p_rows)
        copies.append(
            pltpu.make_async_copy(
                res.at[lax.rem(there_z, 2), half ^ there_x, :, :, part],
                outs[j],
                out_sems.at[j],
            )
        )
    copy_all(copies)


def project(own, other, w_own, w_other, n_tm, p_rows, head_size):
    frames_dev, pos_dev, width = own.shape
    w_rows = w_own.shape[0]
    g_heads = w_rows // head_size
    shape = (g_heads, frames_dev, p_rows, head_size)
    rows = 2 * frames_dev * pos_dev
    return pl.pallas_call(
        functools.partial(project_kernel, n_tm),
        out_shape=[jax.ShapeDtypeStruct(shape, own.dtype)] * n_tm,
        in_specs=[ANY] * 4,
        out_specs=[ANY] * n_tm,
        scratch_shapes=[
            pltpu.VMEM((2, frames_dev, pos_dev, width), jnp.bfloat16),
            pltpu.VMEM((2, w_rows, width), jnp.bfloat16),
            pltpu.VMEM((2, 2, g_heads, frames_dev, pos_dev, head_size), jnp.bfloat16),
            pltpu.SemaphoreType.DMA((2,)),
            pltpu.SemaphoreType.DMA((2,)),
            pltpu.SemaphoreType.DMA((n_tm,)),
        ],
        compiler_params=pltpu.CompilerParams(vmem_limit_bytes=20 * MIB),
        cost_estimate=pl.CostEstimate(
            flops=256 * rows * w_rows * width,
            bytes_accessed=2 * width * (rows + 2 * w_rows),
            transcendentals=0,
        ),
        name="project",
    )(
        pltpu.with_memory_space_constraint(own, pltpu.HBM),
        other,
        pltpu.with_memory_space_constraint(w_own, pltpu.HBM),
        w_other,
    )


def by_position(wide, out, frames, p_rows):
    per = out.shape[1] // frames
    groups = p_rows // per
    for h in range(wide.shape[0]):
        for p in range(p_rows):
            rows = slice(p % per * frames, (p % per + 1) * frames)
            out[h * groups + p // per, rows] = wide[h, pl.ds(p, frames, stride=p_rows), :].astype(
                jnp.bfloat16
            )


def probs_kernel(qkv, *refs):
    by_pos, probs_ref, wide = refs[:3], refs[3], refs[4]
    n_tm, _, frames_dev, g_heads, p_rows, head_size = qkv.shape
    frames = n_tm * frames_dev
    slot_rows = frames_dev * p_rows
    block = probs_ref.shape[-1]
    for a in range(3):
        for h in range(g_heads):
            for k in range(n_tm):
                wide[a, h, k * slot_rows : (k + 1) * slot_rows] = (
                    qkv[k, a, :, h].reshape(slot_rows, head_size).astype(jnp.float32)
                )
        by_position(wide.at[a], by_pos[a], frames, p_rows)
    row = lax.broadcasted_iota(jnp.int32, (1, block, block), 1) // frames
    col = lax.broadcasted_iota(jnp.int32, (1, block, block), 2) // frames
    scores = blocks_dot(by_pos[0][...], by_pos[1][...], 2, 2) * head_size ** (-0.5)
    scores = jnp.where(row == col, scores, -jnp.inf)
    expo = jnp.exp(scores - jnp.max(scores, axis=-1, keepdims=True))
    probs_ref[...] = expo / jnp.sum(expo, axis=-1, keepdims=True)


def grads_kernel(n_tm, slots, *refs):
    gin = refs[:n_tm]
    q_ref, k_ref, v_ref, probs_ref = refs[n_tm : n_tm + 4]
    outs = refs[n_tm + 4 : 2 * n_tm + 4]
    wide, g_ref, back = refs[2 * n_tm + 4 :]
    g_heads, frames_dev, p_rows, head_size = gin[0].shape
    frames = n_tm * frames_dev
    slot_rows = frames_dev * p_rows
    scale = head_size ** (-0.5)
    me, half = lax.axis_index("tm"), lax.axis_index("fsdp") // 2
    for j, r in enumerate(ROUNDS):
        slot = 2 * ((me // 2) ^ (r // 2)) + (half ^ (r % 2))
        rows = pl.ds(pl.multiple_of(slot * slot_rows, slot_rows), slot_rows)
        for h in range(g_heads):
            wide[h, rows] = gin[j][h].reshape(slot_rows, head_size).astype(jnp.float32)
    by_position(wide, g_ref, frames, p_rows)
    g, probs = g_ref[...], probs_ref[...]
    probs_b = probs.astype(jnp.bfloat16)
    dprobs = blocks_dot(g, v_ref[...], 2, 2)
    row_delta = jnp.sum(probs_b.astype(jnp.float32) * dprobs, axis=-1, keepdims=True)
    dscores = (probs * (dprobs - row_delta)).astype(jnp.bfloat16)
    grads = (
        blocks_dot(dscores, k_ref[...], 2, 1) * scale,
        blocks_dot(dscores, q_ref[...], 1, 1) * scale,
        blocks_dot(probs_b, g, 1, 1),
    )
    per = g.shape[1] // frames
    groups = p_rows // per
    for a, grad in enumerate(grads):
        for h in range(g_heads):
            for p in range(p_rows):
                back[a, h, pl.ds(p, frames, stride=p_rows), :] = grad[
                    h * groups + p // per, p % per * frames : (p % per + 1) * frames
                ]
    for a in range(3):
        for h in range(g_heads):
            for k, out in zip(slots, outs):
                rows = pl.ds(pl.multiple_of((me ^ k) * slot_rows, slot_rows), slot_rows)
                out[a, :, h] = (
                    back[a, h, rows]
                    .astype(jnp.bfloat16)
                    .reshape(frames_dev, p_rows, head_size)
                )


def probs_of(qkv):
    n_tm, _, frames_dev, g_heads, p_rows, head_size = qkv.shape
    frames = n_tm * frames_dev
    per = max(1, 128 // frames)
    block = per * frames
    count = g_heads * p_rows // per
    return pl.pallas_call(
        probs_kernel,
        out_shape=[jax.ShapeDtypeStruct((count, block, head_size), jnp.bfloat16)] * 3
        + [jax.ShapeDtypeStruct((count, block, block), jnp.float32)],
        in_specs=[VMEM],
        out_specs=[VMEM] * 4,
        scratch_shapes=[pltpu.VMEM((3, g_heads, frames * p_rows, head_size), jnp.float32)],
        compiler_params=pltpu.CompilerParams(vmem_limit_bytes=16 * MIB),
        name="probs",
    )(qkv)


def grads_of(gin, by_pos, slots, shape):
    n_tm = len(gin)
    _, frames_dev, g_heads, p_rows, head_size = shape
    frames = n_tm * frames_dev
    return pl.pallas_call(
        functools.partial(grads_kernel, n_tm, slots),
        out_shape=[jax.ShapeDtypeStruct(shape, jnp.bfloat16)] * n_tm,
        in_specs=[VMEM] * (n_tm + 4),
        out_specs=[VMEM] * n_tm,
        scratch_shapes=[
            pltpu.VMEM((g_heads, frames * p_rows, head_size), jnp.float32),
            pltpu.VMEM(by_pos[0].shape, jnp.bfloat16),
            pltpu.VMEM((3, g_heads, frames * p_rows, head_size), jnp.float32),
        ],
        compiler_params=pltpu.CompilerParams(vmem_limit_bytes=16 * MIB),
        name="grads",
    )(*gin, *by_pos)


def after(later, earlier):
    return lax.optimization_barrier((later, earlier))


def body_permutes(n_tm, n_fsdp, queries, key_states, value_states, out_grad, out_proj):
    _, pos_dev, _, head_size = queries.shape
    p_rows = pos_dev * GROUPS // n_tm
    slots = SLOTS

    def swap(x, bit):
        return lax.ppermute(x, "fsdp", [(i, i ^ bit) for i in range(n_fsdp)])

    def send(message, k):
        return lax.ppermute(message, "tm", [(i, i ^ k) for i in range(n_tm)]) if k else message

    def round_of(message, r):
        kz, kx = r // 2, r % 2
        pairs = []
        for tm in range(n_tm):
            for fs in range(n_fsdp):
                z, y, x, core = tm // 2, tm % 2, fs // 2, fs % 2
                there = (2 * (z ^ kz) + x) * n_fsdp + 2 * (y ^ kx) + core
                pairs.append((tm * n_fsdp + fs, there))
        return lax.ppermute(message, ("tm", "fsdp"), pairs)

    other = swap(out_grad, 2)
    w_other = swap(out_proj, 1)
    heads_out = lambda x: jnp.transpose(x, (0, 2, 1, 3))
    qkv = lax.all_to_all(
        pack(heads_out(queries), heads_out(key_states), heads_out(value_states), n_tm, p_rows),
        "tm",
        split_axis=0,
        concat_axis=0,
        tiled=True,
    )
    messages = project(out_grad, other, out_proj, w_other, n_tm, p_rows, head_size)
    gin = [round_of(m, r) for r, m in zip(ROUNDS, messages)]
    grads = grads_of(gin, probs_of(qkv), slots, qkv.shape[1:])
    grads = [send(g, k) for g, k in zip(grads, slots)]
    return tuple(heads_out(g) for g in unpack(grads, slots, pos_dev))


def solution(mesh):
    n_tm, n_fsdp = mesh.shape["tm"], mesh.shape["fsdp"]

    def body(queries, key_states, value_states, out_grad, out_proj):
        _, pos_dev, heads, head_size = queries.shape
        fits = (
            n_tm == 2 * GROUPS
            and n_fsdp == GROUPS
            and heads % GROUPS == 0
            and out_proj.shape[0] * GROUPS == heads * head_size
            and pos_dev % 32 == 0
            and head_size == 128
        )
        if fits:
            return body_permutes(
                n_tm, n_fsdp, queries, key_states, value_states, out_grad, out_proj
            )
        return body_any(queries, key_states, value_states, out_grad, out_proj)

    return jax.shard_map(
        body,
        mesh=mesh,
        in_specs=(
            P("tm", "fsdp", None, None),
            P("tm", "fsdp", None, None),
            P("tm", "fsdp", None, None),
            P("tm", "fsdp", None),
            P("fsdp", None),
        ),
        out_specs=(
            P("tm", "fsdp", None, None),
            P("tm", "fsdp", None, None),
            P("tm", "fsdp", None, None),
        ),
        check_vma=False,
    )
```

```python
import functools

import jax
import jax.numpy as jnp
from jax import lax
from jax.experimental import pallas as pl
from jax.experimental.pallas import tpu as pltpu
from jax.sharding import PartitionSpec as P

ANY = pl.BlockSpec(memory_space=pl.ANY)
HBM = pl.BlockSpec(memory_space=pltpu.HBM)
VMEM = pl.BlockSpec(memory_space=pltpu.VMEM)
MIB = 1024 * 1024
SLOTS = (7, 4, 6, 5, 3, 2, 1, 0)
FAR = (7, 4, 6, 5)
ROUNDS = (0, 1, 4, 5, 6, 7, 2, 3)
GROUPS = 4


NT = (((1,), (1,)), ((), ()))
dot = functools.partial(lax.dot_general, preferred_element_type=jnp.float32)


def blocks_dot(a, b, over_a, over_b):
    return dot(a, b, (((over_a,), (over_b,)), ((0,), (0,))))


def attend_back(query_block, key_block, value_block, grad_block):
    score_scale = query_block.shape[-1] ** (-0.5)
    scores = (
        jnp.einsum("fphd,gphd->phfg", query_block, key_block, preferred_element_type=jnp.float32)
        * score_scale
    )
    peak = jnp.max(scores, axis=-1, keepdims=True)
    expo = jnp.exp(scores - peak)
    probs = expo / jnp.sum(expo, axis=-1, keepdims=True)
    probs_b = probs.astype(jnp.bfloat16)
    attn_out = jnp.einsum(
        "phfg,gphd->fphd", probs_b, value_block, preferred_element_type=jnp.float32
    )
    row_delta = jnp.einsum("fphd,fphd->phf", grad_block.astype(jnp.float32), attn_out)
    dprobs = jnp.einsum(
        "fphd,gphd->phfg", grad_block, value_block, preferred_element_type=jnp.float32
    )
    dscores = (probs * (dprobs - row_delta[..., None])).astype(jnp.bfloat16)
    query_grad = (
        jnp.einsum("phfg,gphd->fphd", dscores, key_block, preferred_element_type=jnp.float32)
        * score_scale
    ).astype(jnp.bfloat16)
    key_grad = (
        jnp.einsum("phfg,fphd->gphd", dscores, query_block, preferred_element_type=jnp.float32)
        * score_scale
    ).astype(jnp.bfloat16)
    value_grad = jnp.einsum(
        "phfg,fphd->gphd", probs_b, grad_block, preferred_element_type=jnp.float32
    ).astype(jnp.bfloat16)
    return (query_grad, key_grad, value_grad)


def body_any(queries, key_states, value_states, out_grad, out_proj):
    frames_dev, pos_dev, heads, head_size = queries.shape
    flat = out_grad.reshape(frames_dev * pos_dev, out_grad.shape[-1])
    grad_attn = (
        lax.dot_general(
            flat,
            lax.all_gather(out_proj, "fsdp", axis=0, tiled=True),
            (((1,), (1,)), ((), ())),
            preferred_element_type=jnp.float32,
        )
        .astype(jnp.bfloat16)
        .reshape(frames_dev, pos_dev, heads, head_size)
    )
    there = functools.partial(
        lax.all_to_all, axis_name="tm", split_axis=1, concat_axis=0, tiled=True
    )
    back = functools.partial(
        lax.all_to_all, axis_name="tm", split_axis=0, concat_axis=1, tiled=True
    )
    grads = attend_back(there(queries), there(key_states), there(value_states), there(grad_attn))
    return tuple(back(g) for g in grads)


def group_of(tm):
    return 2 * (tm % 2) + tm // 2 % 2


def part_of(tm):
    return tm // GROUPS


def copy_all(copies):
    for copy in copies:
        copy.start()
    for copy in copies:
        copy.wait()


def pack_copies(there, q_k_v, message, sems):
    _, _, g_heads, p_rows, _ = message.shape
    heads = pl.ds(group_of(there) * g_heads, g_heads)
    rows = pl.ds(pl.multiple_of(part_of(there) * p_rows, p_rows), p_rows)
    return [
        pltpu.make_async_copy(ref.at[:, heads, rows], message.at[a], sems.at[a])
        for a, ref in enumerate(q_k_v)
    ]


def pack_far_kernel(ks, *refs):
    q_k_v, outs, (stage, in_sems, out_sems) = refs[:3], refs[3:-3], refs[-3:]
    me = lax.axis_index("tm")
    arrivals = [
        pack_copies(me ^ k, q_k_v, stage.at[j], in_sems.at[j]) for j, k in enumerate(ks)
    ]
    departures = [
        pltpu.make_async_copy(stage.at[j], out, out_sems.at[j]) for j, out in enumerate(outs)
    ]
    for copies in arrivals:
        for copy in copies:
            copy.start()
    for copies, departure in zip(arrivals, departures):
        for copy in copies:
            copy.wait()
        departure.start()
    for departure in departures:
        departure.wait()


def pack_near_kernel(*refs):
    q_k_v, out, stage, sems = refs[:3], refs[3], refs[4], refs[5]
    first = lax.axis_index("tm") // GROUPS * GROUPS
    copy_all(
        [
            copy
            for j in range(GROUPS)
            for copy in pack_copies(first + j, q_k_v, stage.at[j], sems.at[j])
        ]
    )
    out[...] = stage[...]


def message_shape(q, p_rows):
    frames_dev, heads, _, head_size = q.shape
    return (3, frames_dev, heads // GROUPS, p_rows, head_size)


def pack_far(q_k_v, ks, p_rows):
    shape = message_shape(q_k_v[0], p_rows)
    return pl.pallas_call(
        functools.partial(pack_far_kernel, ks),
        out_shape=[jax.ShapeDtypeStruct(shape, q_k_v[0].dtype)] * len(ks),
        in_specs=[HBM] * 3,
        out_specs=[ANY] * len(ks),
        scratch_shapes=[
            pltpu.VMEM((len(ks),) + shape, q_k_v[0].dtype),
            pltpu.SemaphoreType.DMA((len(ks), 3)),
            pltpu.SemaphoreType.DMA((len(ks),)),
        ],
        compiler_params=pltpu.CompilerParams(vmem_limit_bytes=4 * MIB),
        name="pack_far",
    )(*(pltpu.with_memory_space_constraint(x, pltpu.HBM) for x in q_k_v))


def pack_near(q_k_v, p_rows):
    shape = (GROUPS,) + message_shape(q_k_v[0], p_rows)
    return pl.pallas_call(
        pack_near_kernel,
        out_shape=jax.ShapeDtypeStruct(shape, q_k_v[0].dtype),
        in_specs=[HBM] * 3,
        out_specs=VMEM,
        scratch_shapes=[
            pltpu.VMEM(shape, q_k_v[0].dtype),
            pltpu.SemaphoreType.DMA((GROUPS, 3)),
        ],
        compiler_params=pltpu.CompilerParams(vmem_limit_bytes=4 * MIB),
        name="pack_near",
    )(*(pltpu.with_memory_space_constraint(x, pltpu.HBM) for x in q_k_v))


def unpack_kernel(slots, *refs):
    n_tm = len(slots)
    grads, outs, sems = refs[:n_tm], refs[n_tm : n_tm + 3], refs[n_tm + 3]
    me = lax.axis_index("tm")
    _, _, g_heads, p_rows, _ = grads[0].shape
    copies = []
    for j, k in enumerate(slots):
        there = me ^ k
        heads = pl.ds(group_of(there) * g_heads, g_heads)
        rows = pl.ds(pl.multiple_of(part_of(there) * p_rows, p_rows), p_rows)
        for a, ref in enumerate(outs):
            copies.append(
                pltpu.make_async_copy(grads[j].at[a], ref.at[:, heads, rows], sems.at[3 * j + a])
            )
    copy_all(copies)


def unpack(grads, slots, pos_dev):
    n_tm = len(grads)
    _, frames_dev, g_heads, _, head_size = grads[0].shape
    shape = (frames_dev, g_heads * GROUPS, pos_dev, head_size)
    return pl.pallas_call(
        functools.partial(unpack_kernel, slots),
        out_shape=[jax.ShapeDtypeStruct(shape, grads[0].dtype)] * 3,
        in_specs=[ANY] * n_tm,
        out_specs=[HBM] * 3,
        scratch_shapes=[pltpu.SemaphoreType.DMA((3 * n_tm,))],
        compiler_params=pltpu.CompilerParams(vmem_limit_bytes=1 * MIB),
        name="unpack",
    )(*grads)


def project_into(res, at, w, out):
    g_heads, frames_dev, pos_dev, head_size = res.shape[2:]
    for h in range(g_heads):
        res[w, at, h] = out[:, h * head_size : (h + 1) * head_size].reshape(
            frames_dev, pos_dev, head_size
        )


def flat(rows_ref):
    frames_dev, pos_dev, width = rows_ref.shape
    return rows_ref[...].reshape(frames_dev * pos_dev, width)


def project_own_kernel(own_ref, w_own_ref, w_other_ref, res, w_ref, rows_ref, sems):
    core = lax.rem(lax.axis_index("fsdp"), 2)
    w_copies = [
        pltpu.make_async_copy(ref, w_ref.at[i], sems.at[i])
        for i, ref in enumerate((w_own_ref, w_other_ref))
    ]
    rows_copy = pltpu.make_async_copy(own_ref, rows_ref, sems.at[2])
    for copy in (w_copies[0], rows_copy, w_copies[1]):
        copy.start()
    rows_copy.wait()
    rows = flat(rows_ref)
    for i, copy in enumerate(w_copies):
        copy.wait()
        project_into(res, 0, core ^ i, dot(rows, w_ref[i], NT).astype(jnp.bfloat16))


def project_other_kernel(n_tm, other_ref, w_ref, own_ref, *refs):
    outs, res, sems = refs[:n_tm], refs[n_tm], refs[n_tm + 1]
    me, fs = lax.axis_index("tm"), lax.axis_index("fsdp")
    half, core = fs // 2, lax.rem(fs, 2)
    rows = flat(other_ref)
    for i in range(2):
        project_into(res, 1, core ^ i, dot(rows, w_ref[i], NT).astype(jnp.bfloat16))
    for i in range(2):
        res[i, 0] = own_ref[i, 0]
    p_rows = outs[0].shape[2]
    y, z = lax.rem(me, 2), me // 2
    copies = []
    for j, r in enumerate(ROUNDS):
        there_z, there_x = z ^ (r // 2), y ^ (r % 2)
        part = pl.ds(pl.multiple_of((there_z // 2) * p_rows, p_rows), p_rows)
        copies.append(
            pltpu.make_async_copy(
                res.at[lax.rem(there_z, 2), half ^ there_x, :, :, part],
                outs[j],
                sems.at[j],
            )
        )
    copy_all(copies)


def project_cost(own, w_own, weight):
    rows = own.shape[0] * own.shape[1]
    return pl.CostEstimate(
        flops=weight * 4 * rows * w_own.shape[0] * own.shape[2],
        bytes_accessed=2 * own.shape[2] * (rows + 2 * w_own.shape[0]),
        transcendentals=0,
    )


def project_own(own, w_own, w_other, head_size):
    frames_dev, pos_dev, width = own.shape
    w_rows = w_own.shape[0]
    return pl.pallas_call(
        project_own_kernel,
        out_shape=[
            jax.ShapeDtypeStruct(
                (2, 1, w_rows // head_size, frames_dev, pos_dev, head_size), own.dtype
            ),
            jax.ShapeDtypeStruct((2, w_rows, width), own.dtype),
        ],
        in_specs=[HBM] * 3,
        out_specs=[VMEM] * 2,
        scratch_shapes=[
            pltpu.VMEM(own.shape, own.dtype),
            pltpu.SemaphoreType.DMA((3,)),
        ],
        compiler_params=pltpu.CompilerParams(vmem_limit_bytes=14 * MIB),
        cost_estimate=project_cost(own, w_own, 1),
        name="project_own",
    )(*(pltpu.with_memory_space_constraint(x, pltpu.HBM) for x in (own, w_own, w_other)))


def project_other(other, w, res_own, n_tm, p_rows):
    _, _, g_heads, frames_dev, pos_dev, head_size = res_own.shape
    shape = (g_heads, frames_dev, p_rows, head_size)
    return pl.pallas_call(
        functools.partial(project_other_kernel, n_tm),
        out_shape=[jax.ShapeDtypeStruct(shape, other.dtype)] * n_tm,
        in_specs=[VMEM] * 3,
        out_specs=[ANY] * n_tm,
        scratch_shapes=[
            pltpu.VMEM((2, 2) + res_own.shape[2:], jnp.bfloat16),
            pltpu.SemaphoreType.DMA((n_tm,)),
        ],
        compiler_params=pltpu.CompilerParams(vmem_limit_bytes=14 * MIB),
        cost_estimate=project_cost(other, w[0], 16),
        name="project_other",
    )(other, w, res_own)


def by_position(wide, out, frames, p_rows):
    per = out.shape[1] // frames
    groups = p_rows // per
    for h in range(wide.shape[0]):
        for p in range(p_rows):
            rows = slice(p % per * frames, (p % per + 1) * frames)
            out[h * groups + p // per, rows] = wide[h, pl.ds(p, frames, stride=p_rows), :].astype(
                jnp.bfloat16
            )


def probs_kernel(ks, *refs):
    far, near = refs[: len(ks)], refs[len(ks)]
    by_pos, probs_ref, wide = refs[len(ks) + 1 : len(ks) + 4], refs[len(ks) + 4], refs[-1]
    _, frames_dev, g_heads, p_rows, head_size = far[0].shape
    n_tm = len(ks) + GROUPS
    me = lax.axis_index("tm")
    slots = [(me ^ k, ref) for k, ref in zip(ks, far)]
    slots += [(me // GROUPS * GROUPS + j, near.at[j]) for j in range(GROUPS)]
    frames = n_tm * frames_dev
    slot_rows = frames_dev * p_rows
    block = probs_ref.shape[-1]
    for a in range(3):
        for h in range(g_heads):
            for slot, ref in slots:
                rows = pl.ds(pl.multiple_of(slot * slot_rows, slot_rows), slot_rows)
                wide[a, h, rows] = (
                    ref[a, :, h].reshape(slot_rows, head_size).astype(jnp.float32)
                )
        by_position(wide.at[a], by_pos[a], frames, p_rows)
    row = lax.broadcasted_iota(jnp.int32, (1, block, block), 1) // frames
    col = lax.broadcasted_iota(jnp.int32, (1, block, block), 2) // frames
    scores = blocks_dot(by_pos[0][...], by_pos[1][...], 2, 2) * head_size ** (-0.5)
    scores = jnp.where(row == col, scores, -jnp.inf)
    expo = jnp.exp(scores - jnp.max(scores, axis=-1, keepdims=True))
    probs_ref[...] = expo / jnp.sum(expo, axis=-1, keepdims=True)


def grads_kernel(n_tm, slots, *refs):
    gin = refs[:n_tm]
    q_ref, k_ref, v_ref, probs_ref = refs[n_tm : n_tm + 4]
    outs = refs[n_tm + 4 : 2 * n_tm + 4]
    wide, g_ref, back = refs[2 * n_tm + 4 :]
    g_heads, frames_dev, p_rows, head_size = gin[0].shape
    frames = n_tm * frames_dev
    slot_rows = frames_dev * p_rows
    scale = head_size ** (-0.5)
    me, half = lax.axis_index("tm"), lax.axis_index("fsdp") // 2
    for j, r in enumerate(ROUNDS):
        slot = 2 * ((me // 2) ^ (r // 2)) + (half ^ (r % 2))
        rows = pl.ds(pl.multiple_of(slot * slot_rows, slot_rows), slot_rows)
        for h in range(g_heads):
            wide[h, rows] = gin[j][h].reshape(slot_rows, head_size).astype(jnp.float32)
    by_position(wide, g_ref, frames, p_rows)
    g, probs = g_ref[...], probs_ref[...]
    probs_b = probs.astype(jnp.bfloat16)
    dprobs = blocks_dot(g, v_ref[...], 2, 2)
    row_delta = jnp.sum(probs_b.astype(jnp.float32) * dprobs, axis=-1, keepdims=True)
    dscores = (probs * (dprobs - row_delta)).astype(jnp.bfloat16)
    grads = (
        blocks_dot(dscores, k_ref[...], 2, 1) * scale,
        blocks_dot(dscores, q_ref[...], 1, 1) * scale,
        blocks_dot(probs_b, g, 1, 1),
    )
    per = g.shape[1] // frames
    groups = p_rows // per
    for a, grad in enumerate(grads):
        for h in range(g_heads):
            for p in range(p_rows):
                back[a, h, pl.ds(p, frames, stride=p_rows), :] = grad[
                    h * groups + p // per, p % per * frames : (p % per + 1) * frames
                ]
    for a in range(3):
        for h in range(g_heads):
            for k, out in zip(slots, outs):
                rows = pl.ds(pl.multiple_of((me ^ k) * slot_rows, slot_rows), slot_rows)
                out[a, :, h] = (
                    back[a, h, rows]
                    .astype(jnp.bfloat16)
                    .reshape(frames_dev, p_rows, head_size)
                )


def probs_of(far, near, ks):
    _, frames_dev, g_heads, p_rows, head_size = far[0].shape
    frames = (len(ks) + GROUPS) * frames_dev
    per = max(1, 128 // frames)
    block = per * frames
    count = g_heads * p_rows // per
    return pl.pallas_call(
        functools.partial(probs_kernel, ks),
        out_shape=[jax.ShapeDtypeStruct((count, block, head_size), jnp.bfloat16)] * 3
        + [jax.ShapeDtypeStruct((count, block, block), jnp.float32)],
        in_specs=[VMEM] * (len(ks) + 1),
        out_specs=[VMEM] * 4,
        scratch_shapes=[pltpu.VMEM((3, g_heads, frames * p_rows, head_size), jnp.float32)],
        compiler_params=pltpu.CompilerParams(vmem_limit_bytes=16 * MIB),
        name="probs",
    )(*far, near)


def grads_of(gin, by_pos, slots, shape):
    n_tm = len(gin)
    _, frames_dev, g_heads, p_rows, head_size = shape
    frames = n_tm * frames_dev
    return pl.pallas_call(
        functools.partial(grads_kernel, n_tm, slots),
        out_shape=[jax.ShapeDtypeStruct(shape, jnp.bfloat16)] * n_tm,
        in_specs=[VMEM] * (n_tm + 4),
        out_specs=[VMEM] * n_tm,
        scratch_shapes=[
            pltpu.VMEM((g_heads, frames * p_rows, head_size), jnp.float32),
            pltpu.VMEM(by_pos[0].shape, jnp.bfloat16),
            pltpu.VMEM((3, g_heads, frames * p_rows, head_size), jnp.float32),
        ],
        compiler_params=pltpu.CompilerParams(vmem_limit_bytes=16 * MIB),
        name="grads",
    )(*gin, *by_pos)


def after(later, earlier):
    return lax.optimization_barrier((later, earlier))


def body_permutes(n_tm, n_fsdp, queries, key_states, value_states, out_grad, out_proj):
    _, pos_dev, _, head_size = queries.shape
    p_rows = pos_dev * GROUPS // n_tm
    slots = SLOTS

    def swap(x, bit):
        return lax.ppermute(x, "fsdp", [(i, i ^ bit) for i in range(n_fsdp)])

    def send(message, k):
        return lax.ppermute(message, "tm", [(i, i ^ k) for i in range(n_tm)]) if k else message

    def round_of(message, r):
        kz, kx = r // 2, r % 2
        pairs = []
        for tm in range(n_tm):
            for fs in range(n_fsdp):
                z, y, x, core = tm // 2, tm % 2, fs // 2, fs % 2
                there = (2 * (z ^ kz) + x) * n_fsdp + 2 * (y ^ kx) + core
                pairs.append((tm * n_fsdp + fs, there))
        return lax.ppermute(message, ("tm", "fsdp"), pairs)

    other = swap(out_grad, 2)
    w_other = swap(out_proj, 1)
    heads_out = lambda x: jnp.transpose(x, (0, 2, 1, 3))
    q_k_v = (heads_out(queries), heads_out(key_states), heads_out(value_states))
    far = FAR
    far_messages = list(pack_far(q_k_v, far, p_rows))
    near_message = pack_near(q_k_v, p_rows)
    far_messages[3], w_other = after(far_messages[3], w_other)
    far_qkv = [send(m, k) for m, k in zip(far_messages, far)]
    near_qkv = lax.all_to_all(
        near_message,
        "tm",
        split_axis=0,
        concat_axis=0,
        axis_index_groups=[[b + j for j in range(GROUPS)] for b in range(0, n_tm, GROUPS)],
        tiled=True,
    )
    res_own, w_both = project_own(out_grad, out_proj, w_other, head_size)
    messages = project_other(other, w_both, res_own, n_tm, p_rows)
    gin = [round_of(m, r) for r, m in zip(ROUNDS, messages)]
    grads = grads_of(gin, probs_of(far_qkv, near_qkv, far), slots, far_qkv[0].shape)
    grads = [send(g, k) for g, k in zip(grads, slots)]
    return tuple(heads_out(g) for g in unpack(grads, slots, pos_dev))


def solution(mesh):
    n_tm, n_fsdp = mesh.shape["tm"], mesh.shape["fsdp"]

    def body(queries, key_states, value_states, out_grad, out_proj):
        _, pos_dev, heads, head_size = queries.shape
        fits = (
            n_tm == 2 * GROUPS
            and n_fsdp == GROUPS
            and heads % GROUPS == 0
            and out_proj.shape[0] * GROUPS == heads * head_size
            and pos_dev % 32 == 0
            and head_size == 128
        )
        if fits:
            return body_permutes(
                n_tm, n_fsdp, queries, key_states, value_states, out_grad, out_proj
            )
        return body_any(queries, key_states, value_states, out_grad, out_proj)

    return jax.shard_map(
        body,
        mesh=mesh,
        in_specs=(
            P("tm", "fsdp", None, None),
            P("tm", "fsdp", None, None),
            P("tm", "fsdp", None, None),
            P("tm", "fsdp", None),
            P("fsdp", None),
        ),
        out_specs=(
            P("tm", "fsdp", None, None),
            P("tm", "fsdp", None, None),
            P("tm", "fsdp", None, None),
        ),
        check_vma=False,
    )
```

```python
import functools

import jax
import jax.numpy as jnp
from jax import lax
from jax.experimental import pallas as pl
from jax.experimental.pallas import tpu as pltpu
from jax.sharding import PartitionSpec as P

ANY = pl.BlockSpec(memory_space=pl.ANY)
HBM = pl.BlockSpec(memory_space=pltpu.HBM)
VMEM = pl.BlockSpec(memory_space=pltpu.VMEM)
MIB = 1024 * 1024
SLOTS = (6, 7, 4, 5, 3, 2, 1, 0)
LATE = (4, 5)
FAR = (7, 6, 4, 5)
ROUNDS = (0, 1, 6, 7, 4, 5, 2, 3)
GROUPS = 4


NT = (((1,), (1,)), ((), ()))
dot = functools.partial(lax.dot_general, preferred_element_type=jnp.float32)


def blocks_dot(a, b, over_a, over_b):
    return dot(a, b, (((over_a,), (over_b,)), ((0,), (0,))))


def attend_back(query_block, key_block, value_block, grad_block):
    score_scale = query_block.shape[-1] ** (-0.5)
    scores = (
        jnp.einsum("fphd,gphd->phfg", query_block, key_block, preferred_element_type=jnp.float32)
        * score_scale
    )
    peak = jnp.max(scores, axis=-1, keepdims=True)
    expo = jnp.exp(scores - peak)
    probs = expo / jnp.sum(expo, axis=-1, keepdims=True)
    probs_b = probs.astype(jnp.bfloat16)
    attn_out = jnp.einsum(
        "phfg,gphd->fphd", probs_b, value_block, preferred_element_type=jnp.float32
    )
    row_delta = jnp.einsum("fphd,fphd->phf", grad_block.astype(jnp.float32), attn_out)
    dprobs = jnp.einsum(
        "fphd,gphd->phfg", grad_block, value_block, preferred_element_type=jnp.float32
    )
    dscores = (probs * (dprobs - row_delta[..., None])).astype(jnp.bfloat16)
    query_grad = (
        jnp.einsum("phfg,gphd->fphd", dscores, key_block, preferred_element_type=jnp.float32)
        * score_scale
    ).astype(jnp.bfloat16)
    key_grad = (
        jnp.einsum("phfg,fphd->gphd", dscores, query_block, preferred_element_type=jnp.float32)
        * score_scale
    ).astype(jnp.bfloat16)
    value_grad = jnp.einsum(
        "phfg,fphd->gphd", probs_b, grad_block, preferred_element_type=jnp.float32
    ).astype(jnp.bfloat16)
    return (query_grad, key_grad, value_grad)


def body_any(queries, key_states, value_states, out_grad, out_proj):
    frames_dev, pos_dev, heads, head_size = queries.shape
    flat = out_grad.reshape(frames_dev * pos_dev, out_grad.shape[-1])
    grad_attn = (
        lax.dot_general(
            flat,
            lax.all_gather(out_proj, "fsdp", axis=0, tiled=True),
            (((1,), (1,)), ((), ())),
            preferred_element_type=jnp.float32,
        )
        .astype(jnp.bfloat16)
        .reshape(frames_dev, pos_dev, heads, head_size)
    )
    there = functools.partial(
        lax.all_to_all, axis_name="tm", split_axis=1, concat_axis=0, tiled=True
    )
    back = functools.partial(
        lax.all_to_all, axis_name="tm", split_axis=0, concat_axis=1, tiled=True
    )
    grads = attend_back(there(queries), there(key_states), there(value_states), there(grad_attn))
    return tuple(back(g) for g in grads)


def group_of(tm):
    return 2 * (tm % 2) + tm // 2 % 2


def part_of(tm):
    return tm // GROUPS


def copy_all(copies):
    for copy in copies:
        copy.start()
    for copy in copies:
        copy.wait()


def pack_copies(there, q_k_v, message, sems):
    _, _, g_heads, p_rows, _ = message.shape
    heads = pl.ds(group_of(there) * g_heads, g_heads)
    rows = pl.ds(pl.multiple_of(part_of(there) * p_rows, p_rows), p_rows)
    return [
        pltpu.make_async_copy(ref.at[:, heads, rows], message.at[a], sems.at[a])
        for a, ref in enumerate(q_k_v)
    ]


def pack_far_kernel(ks, *refs):
    q_k_v, outs, (stage, in_sems, out_sems) = refs[:3], refs[3:-3], refs[-3:]
    me = lax.axis_index("tm")
    arrivals = [
        pack_copies(me ^ k, q_k_v, stage.at[j], in_sems.at[j]) for j, k in enumerate(ks)
    ]
    departures = [
        pltpu.make_async_copy(stage.at[j], out, out_sems.at[j]) for j, out in enumerate(outs)
    ]
    for copies in arrivals:
        for copy in copies:
            copy.start()
    for copies, departure in zip(arrivals, departures):
        for copy in copies:
            copy.wait()
        departure.start()
    for departure in departures:
        departure.wait()


def pack_near_kernel(*refs):
    q_k_v, out, stage, sems = refs[:3], refs[3], refs[4], refs[5]
    first = lax.axis_index("tm") // GROUPS * GROUPS
    copy_all(
        [
            copy
            for j in range(GROUPS)
            for copy in pack_copies(first + j, q_k_v, stage.at[j], sems.at[j])
        ]
    )
    out[...] = stage[...]


def message_shape(q, p_rows):
    frames_dev, heads, _, head_size = q.shape
    return (3, frames_dev, heads // GROUPS, p_rows, head_size)


def pack_far(q_k_v, ks, p_rows):
    shape = message_shape(q_k_v[0], p_rows)
    return pl.pallas_call(
        functools.partial(pack_far_kernel, ks),
        out_shape=[jax.ShapeDtypeStruct(shape, q_k_v[0].dtype)] * len(ks),
        in_specs=[HBM] * 3,
        out_specs=[ANY] * len(ks),
        scratch_shapes=[
            pltpu.VMEM((len(ks),) + shape, q_k_v[0].dtype),
            pltpu.SemaphoreType.DMA((len(ks), 3)),
            pltpu.SemaphoreType.DMA((len(ks),)),
        ],
        compiler_params=pltpu.CompilerParams(vmem_limit_bytes=4 * MIB),
        name="pack_far",
    )(*(pltpu.with_memory_space_constraint(x, pltpu.HBM) for x in q_k_v))


def pack_near(q_k_v, p_rows):
    shape = (GROUPS,) + message_shape(q_k_v[0], p_rows)
    return pl.pallas_call(
        pack_near_kernel,
        out_shape=jax.ShapeDtypeStruct(shape, q_k_v[0].dtype),
        in_specs=[HBM] * 3,
        out_specs=VMEM,
        scratch_shapes=[
            pltpu.VMEM(shape, q_k_v[0].dtype),
            pltpu.SemaphoreType.DMA((GROUPS, 3)),
        ],
        compiler_params=pltpu.CompilerParams(vmem_limit_bytes=4 * MIB),
        name="pack_near",
    )(*(pltpu.with_memory_space_constraint(x, pltpu.HBM) for x in q_k_v))


def unpack_kernel(ks, *refs):
    grads, outs, sems = refs[: len(ks)], refs[-4:-1], refs[-1]
    me = lax.axis_index("tm")
    _, _, g_heads, p_rows, _ = grads[0].shape
    copies = []
    for j, k in enumerate(ks):
        there = me ^ k
        heads = pl.ds(group_of(there) * g_heads, g_heads)
        rows = pl.ds(pl.multiple_of(part_of(there) * p_rows, p_rows), p_rows)
        for a, ref in enumerate(outs):
            copies.append(
                pltpu.make_async_copy(grads[j].at[a], ref.at[:, heads, rows], sems.at[j, a])
            )
    copy_all(copies)


def unpack(grads, ks, pos_dev, before=()):
    _, frames_dev, g_heads, _, head_size = grads[0].shape
    shape = (frames_dev, g_heads * GROUPS, pos_dev, head_size)
    n = len(ks)
    return pl.pallas_call(
        functools.partial(unpack_kernel, ks),
        out_shape=[jax.ShapeDtypeStruct(shape, grads[0].dtype)] * 3,
        in_specs=[ANY] * n + [HBM] * len(before),
        out_specs=[HBM] * 3,
        scratch_shapes=[pltpu.SemaphoreType.DMA((n, 3))],
        input_output_aliases={n + a: a for a in range(len(before))},
        compiler_params=pltpu.CompilerParams(vmem_limit_bytes=1 * MIB),
        name="unpack",
    )(*grads, *before)


def project_into(res, at, w, out):
    g_heads, frames_dev, pos_dev, head_size = res.shape[2:]
    for h in range(g_heads):
        res[w, at, h] = out[:, h * head_size : (h + 1) * head_size].reshape(
            frames_dev, pos_dev, head_size
        )


def flat(rows_ref):
    frames_dev, pos_dev, width = rows_ref.shape
    return rows_ref[...].reshape(frames_dev * pos_dev, width)


def project_own_kernel(own_ref, w_own_ref, w_other_ref, res, w_ref, rows_ref, sems):
    core = lax.rem(lax.axis_index("fsdp"), 2)
    w_copies = [
        pltpu.make_async_copy(ref, w_ref.at[i], sems.at[i])
        for i, ref in enumerate((w_own_ref, w_other_ref))
    ]
    rows_copy = pltpu.make_async_copy(own_ref, rows_ref, sems.at[2])
    for copy in (w_copies[0], rows_copy, w_copies[1]):
        copy.start()
    rows_copy.wait()
    rows = flat(rows_ref)
    for i, copy in enumerate(w_copies):
        copy.wait()
        project_into(res, 0, core ^ i, dot(rows, w_ref[i], NT).astype(jnp.bfloat16))


def project_other_kernel(n_tm, other_ref, w_ref, own_ref, *refs):
    outs, res, sems = refs[:n_tm], refs[n_tm], refs[n_tm + 1]
    me, fs = lax.axis_index("tm"), lax.axis_index("fsdp")
    half, core = fs // 2, lax.rem(fs, 2)
    rows = flat(other_ref)
    for i in range(2):
        project_into(res, 1, core ^ i, dot(rows, w_ref[i], NT).astype(jnp.bfloat16))
    for i in range(2):
        res[i, 0] = own_ref[i, 0]
    p_rows = outs[0].shape[2]
    y, z = lax.rem(me, 2), me // 2
    copies = []
    for j, r in enumerate(ROUNDS):
        there_z, there_x = z ^ (r // 2), y ^ (r % 2)
        part = pl.ds(pl.multiple_of((there_z // 2) * p_rows, p_rows), p_rows)
        copies.append(
            pltpu.make_async_copy(
                res.at[lax.rem(there_z, 2), half ^ there_x, :, :, part],
                outs[j],
                sems.at[j],
            )
        )
    copy_all(copies)


def project_cost(own, w_own, weight):
    rows = own.shape[0] * own.shape[1]
    return pl.CostEstimate(
        flops=weight * 4 * rows * w_own.shape[0] * own.shape[2],
        bytes_accessed=2 * own.shape[2] * (rows + 2 * w_own.shape[0]),
        transcendentals=0,
    )


def project_own(own, w_own, w_other, head_size):
    frames_dev, pos_dev, width = own.shape
    w_rows = w_own.shape[0]
    return pl.pallas_call(
        project_own_kernel,
        out_shape=[
            jax.ShapeDtypeStruct(
                (2, 1, w_rows // head_size, frames_dev, pos_dev, head_size), own.dtype
            ),
            jax.ShapeDtypeStruct((2, w_rows, width), own.dtype),
        ],
        in_specs=[HBM] * 3,
        out_specs=[VMEM] * 2,
        scratch_shapes=[
            pltpu.VMEM(own.shape, own.dtype),
            pltpu.SemaphoreType.DMA((3,)),
        ],
        compiler_params=pltpu.CompilerParams(vmem_limit_bytes=14 * MIB),
        cost_estimate=project_cost(own, w_own, 1),
        name="project_own",
    )(*(pltpu.with_memory_space_constraint(x, pltpu.HBM) for x in (own, w_own, w_other)))


def project_other(other, w, res_own, n_tm, p_rows):
    _, _, g_heads, frames_dev, pos_dev, head_size = res_own.shape
    shape = (g_heads, frames_dev, p_rows, head_size)
    return pl.pallas_call(
        functools.partial(project_other_kernel, n_tm),
        out_shape=[jax.ShapeDtypeStruct(shape, other.dtype)] * n_tm,
        in_specs=[VMEM] * 3,
        out_specs=[ANY] * n_tm,
        scratch_shapes=[
            pltpu.VMEM((2, 2) + res_own.shape[2:], jnp.bfloat16),
            pltpu.SemaphoreType.DMA((n_tm,)),
        ],
        compiler_params=pltpu.CompilerParams(vmem_limit_bytes=14 * MIB),
        cost_estimate=project_cost(other, w[0], 16),
        name="project_other",
    )(other, w, res_own)


def by_position(wide, out, frames, p_rows):
    per = out.shape[1] // frames
    groups = p_rows // per
    for h in range(wide.shape[0]):
        for p in range(p_rows):
            rows = slice(p % per * frames, (p % per + 1) * frames)
            out[h * groups + p // per, rows] = wide[h, pl.ds(p, frames, stride=p_rows), :].astype(
                jnp.bfloat16
            )


def probs_kernel(ks, *refs):
    far, near = refs[: len(ks)], refs[len(ks)]
    by_pos, probs_ref, wide = refs[len(ks) + 1 : len(ks) + 4], refs[len(ks) + 4], refs[-1]
    _, frames_dev, g_heads, p_rows, head_size = far[0].shape
    n_tm = len(ks) + GROUPS
    me = lax.axis_index("tm")
    slots = [(me ^ k, ref) for k, ref in zip(ks, far)]
    slots += [(me // GROUPS * GROUPS + j, near.at[j]) for j in range(GROUPS)]
    frames = n_tm * frames_dev
    slot_rows = frames_dev * p_rows
    block = probs_ref.shape[-1]
    for a in range(3):
        for h in range(g_heads):
            for slot, ref in slots:
                rows = pl.ds(pl.multiple_of(slot * slot_rows, slot_rows), slot_rows)
                wide[a, h, rows] = (
                    ref[a, :, h].reshape(slot_rows, head_size).astype(jnp.float32)
                )
        by_position(wide.at[a], by_pos[a], frames, p_rows)
    row = lax.broadcasted_iota(jnp.int32, (1, block, block), 1) // frames
    col = lax.broadcasted_iota(jnp.int32, (1, block, block), 2) // frames
    scores = blocks_dot(by_pos[0][...], by_pos[1][...], 2, 2) * head_size ** (-0.5)
    scores = jnp.where(row == col, scores, -jnp.inf)
    expo = jnp.exp(scores - jnp.max(scores, axis=-1, keepdims=True))
    probs_ref[...] = expo / jnp.sum(expo, axis=-1, keepdims=True)


def grads_kernel(n_tm, slots, *refs):
    gin = refs[:n_tm]
    q_ref, k_ref, v_ref, probs_ref = refs[n_tm : n_tm + 4]
    outs = refs[n_tm + 4 : 2 * n_tm + 4]
    wide, g_ref, back = refs[2 * n_tm + 4 :]
    g_heads, frames_dev, p_rows, head_size = gin[0].shape
    frames = n_tm * frames_dev
    slot_rows = frames_dev * p_rows
    scale = head_size ** (-0.5)
    me, half = lax.axis_index("tm"), lax.axis_index("fsdp") // 2
    for j, r in enumerate(ROUNDS):
        slot = 2 * ((me // 2) ^ (r // 2)) + (half ^ (r % 2))
        rows = pl.ds(pl.multiple_of(slot * slot_rows, slot_rows), slot_rows)
        for h in range(g_heads):
            wide[h, rows] = gin[j][h].reshape(slot_rows, head_size).astype(jnp.float32)
    by_position(wide, g_ref, frames, p_rows)
    g, probs = g_ref[...], probs_ref[...]
    probs_b = probs.astype(jnp.bfloat16)
    dprobs = blocks_dot(g, v_ref[...], 2, 2)
    row_delta = jnp.sum(probs_b.astype(jnp.float32) * dprobs, axis=-1, keepdims=True)
    dscores = (probs * (dprobs - row_delta)).astype(jnp.bfloat16)
    grads = (
        blocks_dot(dscores, k_ref[...], 2, 1) * scale,
        blocks_dot(dscores, q_ref[...], 1, 1) * scale,
        blocks_dot(probs_b, g, 1, 1),
    )
    per = g.shape[1] // frames
    groups = p_rows // per
    for a, grad in enumerate(grads):
        for h in range(g_heads):
            for p in range(p_rows):
                back[a, h, pl.ds(p, frames, stride=p_rows), :] = grad[
                    h * groups + p // per, p % per * frames : (p % per + 1) * frames
                ]
    for a in range(3):
        for h in range(g_heads):
            for k, out in zip(slots, outs):
                rows = pl.ds(pl.multiple_of((me ^ k) * slot_rows, slot_rows), slot_rows)
                out[a, :, h] = (
                    back[a, h, rows]
                    .astype(jnp.bfloat16)
                    .reshape(frames_dev, p_rows, head_size)
                )


def probs_of(far, near, ks):
    _, frames_dev, g_heads, p_rows, head_size = far[0].shape
    frames = (len(ks) + GROUPS) * frames_dev
    per = max(1, 128 // frames)
    block = per * frames
    count = g_heads * p_rows // per
    return pl.pallas_call(
        functools.partial(probs_kernel, ks),
        out_shape=[jax.ShapeDtypeStruct((count, block, head_size), jnp.bfloat16)] * 3
        + [jax.ShapeDtypeStruct((count, block, block), jnp.float32)],
        in_specs=[VMEM] * (len(ks) + 1),
        out_specs=[VMEM] * 4,
        scratch_shapes=[pltpu.VMEM((3, g_heads, frames * p_rows, head_size), jnp.float32)],
        compiler_params=pltpu.CompilerParams(vmem_limit_bytes=16 * MIB),
        name="probs",
    )(*far, near)


def grads_of(gin, by_pos, slots, shape):
    n_tm = len(gin)
    _, frames_dev, g_heads, p_rows, head_size = shape
    frames = n_tm * frames_dev
    return pl.pallas_call(
        functools.partial(grads_kernel, n_tm, slots),
        out_shape=[jax.ShapeDtypeStruct(shape, jnp.bfloat16)] * n_tm,
        in_specs=[VMEM] * (n_tm + 4),
        out_specs=[VMEM] * n_tm,
        scratch_shapes=[
            pltpu.VMEM((g_heads, frames * p_rows, head_size), jnp.float32),
            pltpu.VMEM(by_pos[0].shape, jnp.bfloat16),
            pltpu.VMEM((3, g_heads, frames * p_rows, head_size), jnp.float32),
        ],
        compiler_params=pltpu.CompilerParams(vmem_limit_bytes=16 * MIB),
        name="grads",
    )(*gin, *by_pos)


def after(later, earlier):
    return lax.optimization_barrier((later, earlier))


def body_permutes(n_tm, n_fsdp, queries, key_states, value_states, out_grad, out_proj):
    _, pos_dev, _, head_size = queries.shape
    p_rows = pos_dev * GROUPS // n_tm
    slots = SLOTS

    def swap(x, bit):
        return lax.ppermute(x, "fsdp", [(i, i ^ bit) for i in range(n_fsdp)])

    def send(message, k):
        return lax.ppermute(message, "tm", [(i, i ^ k) for i in range(n_tm)]) if k else message

    def round_of(message, r):
        kz, kx = r // 2, r % 2
        pairs = []
        for tm in range(n_tm):
            for fs in range(n_fsdp):
                z, y, x, core = tm // 2, tm % 2, fs // 2, fs % 2
                there = (2 * (z ^ kz) + x) * n_fsdp + 2 * (y ^ kx) + core
                pairs.append((tm * n_fsdp + fs, there))
        return lax.ppermute(message, ("tm", "fsdp"), pairs)

    other = swap(out_grad, 2)
    w_other = swap(out_proj, 1)
    heads_out = lambda x: jnp.transpose(x, (0, 2, 1, 3))
    q_k_v = (heads_out(queries), heads_out(key_states), heads_out(value_states))
    far = FAR
    far_messages = list(pack_far(q_k_v, far, p_rows))
    near_message = pack_near(q_k_v, p_rows)
    far_messages[3], w_other = after(far_messages[3], w_other)
    far_qkv = [send(m, k) for m, k in zip(far_messages, far)]
    near_qkv = lax.all_to_all(
        near_message,
        "tm",
        split_axis=0,
        concat_axis=0,
        axis_index_groups=[[b + j for j in range(GROUPS)] for b in range(0, n_tm, GROUPS)],
        tiled=True,
    )
    res_own, w_both = project_own(out_grad, out_proj, w_other, head_size)
    messages = project_other(other, w_both, res_own, n_tm, p_rows)
    gin = [round_of(m, r) for r, m in zip(ROUNDS, messages)]
    grads = grads_of(gin, probs_of(far_qkv, near_qkv, far), slots, far_qkv[0].shape)
    grads = [send(g, k) for g, k in zip(grads, slots)]
    grads = dict(zip(slots, grads))
    early = tuple(k for k in slots if k not in LATE)
    outs = unpack([grads[k] for k in early], early, pos_dev)
    outs = unpack([grads[k] for k in LATE], LATE, pos_dev, outs)
    return tuple(heads_out(g) for g in outs)


def solution(mesh):
    n_tm, n_fsdp = mesh.shape["tm"], mesh.shape["fsdp"]

    def body(queries, key_states, value_states, out_grad, out_proj):
        _, pos_dev, heads, head_size = queries.shape
        fits = (
            n_tm == 2 * GROUPS
            and n_fsdp == GROUPS
            and heads % GROUPS == 0
            and out_proj.shape[0] * GROUPS == heads * head_size
            and pos_dev % 32 == 0
            and head_size == 128
        )
        if fits:
            return body_permutes(
                n_tm, n_fsdp, queries, key_states, value_states, out_grad, out_proj
            )
        return body_any(queries, key_states, value_states, out_grad, out_proj)

    return jax.shard_map(
        body,
        mesh=mesh,
        in_specs=(
            P("tm", "fsdp", None, None),
            P("tm", "fsdp", None, None),
            P("tm", "fsdp", None, None),
            P("tm", "fsdp", None),
            P("fsdp", None),
        ),
        out_specs=(
            P("tm", "fsdp", None, None),
            P("tm", "fsdp", None, None),
            P("tm", "fsdp", None, None),
        ),
        check_vma=False,
    )
```

```python
import functools

import jax
import jax.numpy as jnp
from jax import lax
from jax.experimental import pallas as pl
from jax.experimental.pallas import tpu as pltpu
from jax.sharding import PartitionSpec as P

ANY = pl.BlockSpec(memory_space=pl.ANY)
HBM = pl.BlockSpec(memory_space=pltpu.HBM)
VMEM = pl.BlockSpec(memory_space=pltpu.VMEM)
MIB = 1024 * 1024
SLOTS = (6, 7, 4, 5, 3, 2, 1, 0)
LATE = (5, 4)
FAR = (7, 6, 4, 5)
ROUNDS = (0, 1, 6, 7, 4, 5, 2, 3)
GROUPS = 4


NT = (((1,), (1,)), ((), ()))
dot = functools.partial(lax.dot_general, preferred_element_type=jnp.float32)


def blocks_dot(a, b, over_a, over_b):
    return dot(a, b, (((over_a,), (over_b,)), ((0,), (0,))))


def attend_back(query_block, key_block, value_block, grad_block):
    score_scale = query_block.shape[-1] ** (-0.5)
    scores = (
        jnp.einsum("fphd,gphd->phfg", query_block, key_block, preferred_element_type=jnp.float32)
        * score_scale
    )
    peak = jnp.max(scores, axis=-1, keepdims=True)
    expo = jnp.exp(scores - peak)
    probs = expo / jnp.sum(expo, axis=-1, keepdims=True)
    probs_b = probs.astype(jnp.bfloat16)
    attn_out = jnp.einsum(
        "phfg,gphd->fphd", probs_b, value_block, preferred_element_type=jnp.float32
    )
    row_delta = jnp.einsum("fphd,fphd->phf", grad_block.astype(jnp.float32), attn_out)
    dprobs = jnp.einsum(
        "fphd,gphd->phfg", grad_block, value_block, preferred_element_type=jnp.float32
    )
    dscores = (probs * (dprobs - row_delta[..., None])).astype(jnp.bfloat16)
    query_grad = (
        jnp.einsum("phfg,gphd->fphd", dscores, key_block, preferred_element_type=jnp.float32)
        * score_scale
    ).astype(jnp.bfloat16)
    key_grad = (
        jnp.einsum("phfg,fphd->gphd", dscores, query_block, preferred_element_type=jnp.float32)
        * score_scale
    ).astype(jnp.bfloat16)
    value_grad = jnp.einsum(
        "phfg,fphd->gphd", probs_b, grad_block, preferred_element_type=jnp.float32
    ).astype(jnp.bfloat16)
    return (query_grad, key_grad, value_grad)


def body_any(queries, key_states, value_states, out_grad, out_proj):
    frames_dev, pos_dev, heads, head_size = queries.shape
    flat = out_grad.reshape(frames_dev * pos_dev, out_grad.shape[-1])
    grad_attn = (
        lax.dot_general(
            flat,
            lax.all_gather(out_proj, "fsdp", axis=0, tiled=True),
            (((1,), (1,)), ((), ())),
            preferred_element_type=jnp.float32,
        )
        .astype(jnp.bfloat16)
        .reshape(frames_dev, pos_dev, heads, head_size)
    )
    there = functools.partial(
        lax.all_to_all, axis_name="tm", split_axis=1, concat_axis=0, tiled=True
    )
    back = functools.partial(
        lax.all_to_all, axis_name="tm", split_axis=0, concat_axis=1, tiled=True
    )
    grads = attend_back(there(queries), there(key_states), there(value_states), there(grad_attn))
    return tuple(back(g) for g in grads)


def group_of(tm):
    return 2 * (tm % 2) + tm // 2 % 2


def part_of(tm):
    return tm // GROUPS


def copy_all(copies):
    for copy in copies:
        copy.start()
    for copy in copies:
        copy.wait()


def pack_copies(there, q_k_v, message, sems):
    _, _, g_heads, p_rows, _ = message.shape
    heads = pl.ds(group_of(there) * g_heads, g_heads)
    rows = pl.ds(pl.multiple_of(part_of(there) * p_rows, p_rows), p_rows)
    return [
        pltpu.make_async_copy(ref.at[:, heads, rows], message.at[a], sems.at[a])
        for a, ref in enumerate(q_k_v)
    ]


def pack_far_kernel(ks, *refs):
    q_k_v, outs, (stage, in_sems, out_sems) = refs[:3], refs[3:-3], refs[-3:]
    me = lax.axis_index("tm")
    arrivals = [
        pack_copies(me ^ k, q_k_v, stage.at[j], in_sems.at[j]) for j, k in enumerate(ks)
    ]
    departures = [
        pltpu.make_async_copy(stage.at[j], out, out_sems.at[j]) for j, out in enumerate(outs)
    ]
    for copies in arrivals:
        for copy in copies:
            copy.start()
    for copies, departure in zip(arrivals, departures):
        for copy in copies:
            copy.wait()
        departure.start()
    for departure in departures:
        departure.wait()


def pack_near_kernel(*refs):
    q_k_v, out, stage, sems = refs[:3], refs[3], refs[4], refs[5]
    first = lax.axis_index("tm") // GROUPS * GROUPS
    copy_all(
        [
            copy
            for j in range(GROUPS)
            for copy in pack_copies(first + j, q_k_v, stage.at[j], sems.at[j])
        ]
    )
    out[...] = stage[...]


def message_shape(q, p_rows):
    frames_dev, heads, _, head_size = q.shape
    return (3, frames_dev, heads // GROUPS, p_rows, head_size)


def pack_far(q_k_v, ks, p_rows):
    shape = message_shape(q_k_v[0], p_rows)
    return pl.pallas_call(
        functools.partial(pack_far_kernel, ks),
        out_shape=[jax.ShapeDtypeStruct(shape, q_k_v[0].dtype)] * len(ks),
        in_specs=[HBM] * 3,
        out_specs=[ANY] * len(ks),
        scratch_shapes=[
            pltpu.VMEM((len(ks),) + shape, q_k_v[0].dtype),
            pltpu.SemaphoreType.DMA((len(ks), 3)),
            pltpu.SemaphoreType.DMA((len(ks),)),
        ],
        compiler_params=pltpu.CompilerParams(vmem_limit_bytes=4 * MIB),
        name="pack_far",
    )(*(pltpu.with_memory_space_constraint(x, pltpu.HBM) for x in q_k_v))


def pack_near(q_k_v, p_rows):
    shape = (GROUPS,) + message_shape(q_k_v[0], p_rows)
    return pl.pallas_call(
        pack_near_kernel,
        out_shape=jax.ShapeDtypeStruct(shape, q_k_v[0].dtype),
        in_specs=[HBM] * 3,
        out_specs=VMEM,
        scratch_shapes=[
            pltpu.VMEM(shape, q_k_v[0].dtype),
            pltpu.SemaphoreType.DMA((GROUPS, 3)),
        ],
        compiler_params=pltpu.CompilerParams(vmem_limit_bytes=4 * MIB),
        name="pack_near",
    )(*(pltpu.with_memory_space_constraint(x, pltpu.HBM) for x in q_k_v))


def unpack_kernel(ks, *refs):
    grads, outs, sems = refs[: len(ks)], refs[-4:-1], refs[-1]
    me = lax.axis_index("tm")
    _, _, g_heads, p_rows, _ = grads[0].shape
    copies = []
    for j, k in enumerate(ks):
        there = me ^ k
        heads = pl.ds(group_of(there) * g_heads, g_heads)
        rows = pl.ds(pl.multiple_of(part_of(there) * p_rows, p_rows), p_rows)
        for a, ref in enumerate(outs):
            copies.append(
                pltpu.make_async_copy(grads[j].at[a], ref.at[:, heads, rows], sems.at[j, a])
            )
    copy_all(copies)


def unpack(grads, ks, pos_dev, before=()):
    _, frames_dev, g_heads, _, head_size = grads[0].shape
    shape = (frames_dev, g_heads * GROUPS, pos_dev, head_size)
    n = len(ks)
    return pl.pallas_call(
        functools.partial(unpack_kernel, ks),
        out_shape=[jax.ShapeDtypeStruct(shape, grads[0].dtype)] * 3,
        in_specs=[ANY] * n + [HBM] * len(before),
        out_specs=[HBM] * 3,
        scratch_shapes=[pltpu.SemaphoreType.DMA((n, 3))],
        input_output_aliases={n + a: a for a in range(len(before))},
        compiler_params=pltpu.CompilerParams(vmem_limit_bytes=1 * MIB),
        name="unpack",
    )(*grads, *before)


def project_into(res, at, w, out):
    g_heads, frames_dev, pos_dev, head_size = res.shape[2:]
    for h in range(g_heads):
        res[w, at, h] = out[:, h * head_size : (h + 1) * head_size].reshape(
            frames_dev, pos_dev, head_size
        )


def flat(rows_ref):
    frames_dev, pos_dev, width = rows_ref.shape
    return rows_ref[...].reshape(frames_dev * pos_dev, width)


def project_own_kernel(own_ref, w_own_ref, w_other_ref, res, w_ref, rows_ref, sems):
    core = lax.rem(lax.axis_index("fsdp"), 2)
    w_copies = [
        pltpu.make_async_copy(ref, w_ref.at[i], sems.at[i])
        for i, ref in enumerate((w_own_ref, w_other_ref))
    ]
    rows_copy = pltpu.make_async_copy(own_ref, rows_ref, sems.at[2])
    for copy in (w_copies[0], rows_copy, w_copies[1]):
        copy.start()
    rows_copy.wait()
    rows = flat(rows_ref)
    for i, copy in enumerate(w_copies):
        copy.wait()
        project_into(res, 0, core ^ i, dot(rows, w_ref[i], NT).astype(jnp.bfloat16))


def project_other_kernel(n_tm, other_ref, w_ref, own_ref, *refs):
    outs, res, sems = refs[:n_tm], refs[n_tm], refs[n_tm + 1]
    me, fs = lax.axis_index("tm"), lax.axis_index("fsdp")
    half, core = fs // 2, lax.rem(fs, 2)
    rows = flat(other_ref)
    for i in range(2):
        project_into(res, 1, core ^ i, dot(rows, w_ref[i], NT).astype(jnp.bfloat16))
    for i in range(2):
        res[i, 0] = own_ref[i, 0]
    p_rows = outs[0].shape[2]
    y, z = lax.rem(me, 2), me // 2
    copies = []
    for j, r in enumerate(ROUNDS):
        there_z, there_x = z ^ (r // 2), y ^ (r % 2)
        part = pl.ds(pl.multiple_of((there_z // 2) * p_rows, p_rows), p_rows)
        copies.append(
            pltpu.make_async_copy(
                res.at[lax.rem(there_z, 2), half ^ there_x, :, :, part],
                outs[j],
                sems.at[j],
            )
        )
    copy_all(copies)


def project_cost(own, w_own, weight):
    rows = own.shape[0] * own.shape[1]
    return pl.CostEstimate(
        flops=weight * 4 * rows * w_own.shape[0] * own.shape[2],
        bytes_accessed=2 * own.shape[2] * (rows + 2 * w_own.shape[0]),
        transcendentals=0,
    )


def project_own(own, w_own, w_other, head_size):
    frames_dev, pos_dev, width = own.shape
    w_rows = w_own.shape[0]
    return pl.pallas_call(
        project_own_kernel,
        out_shape=[
            jax.ShapeDtypeStruct(
                (2, 1, w_rows // head_size, frames_dev, pos_dev, head_size), own.dtype
            ),
            jax.ShapeDtypeStruct((2, w_rows, width), own.dtype),
        ],
        in_specs=[HBM] * 3,
        out_specs=[VMEM] * 2,
        scratch_shapes=[
            pltpu.VMEM(own.shape, own.dtype),
            pltpu.SemaphoreType.DMA((3,)),
        ],
        compiler_params=pltpu.CompilerParams(vmem_limit_bytes=14 * MIB),
        cost_estimate=project_cost(own, w_own, 1),
        name="project_own",
    )(*(pltpu.with_memory_space_constraint(x, pltpu.HBM) for x in (own, w_own, w_other)))


def project_other(other, w, res_own, n_tm, p_rows):
    _, _, g_heads, frames_dev, pos_dev, head_size = res_own.shape
    shape = (g_heads, frames_dev, p_rows, head_size)
    return pl.pallas_call(
        functools.partial(project_other_kernel, n_tm),
        out_shape=[jax.ShapeDtypeStruct(shape, other.dtype)] * n_tm,
        in_specs=[VMEM] * 3,
        out_specs=[ANY] * n_tm,
        scratch_shapes=[
            pltpu.VMEM((2, 2) + res_own.shape[2:], jnp.bfloat16),
            pltpu.SemaphoreType.DMA((n_tm,)),
        ],
        compiler_params=pltpu.CompilerParams(vmem_limit_bytes=14 * MIB),
        cost_estimate=project_cost(other, w[0], 16),
        name="project_other",
    )(other, w, res_own)


def by_position(wide, out, frames, p_rows):
    per = out.shape[1] // frames
    groups = p_rows // per
    for h in range(wide.shape[0]):
        for p in range(p_rows):
            rows = slice(p % per * frames, (p % per + 1) * frames)
            out[h * groups + p // per, rows] = wide[h, pl.ds(p, frames, stride=p_rows), :].astype(
                jnp.bfloat16
            )


def probs_kernel(ks, *refs):
    far, near = refs[: len(ks)], refs[len(ks)]
    by_pos, probs_ref, wide = refs[len(ks) + 1 : len(ks) + 4], refs[len(ks) + 4], refs[-1]
    _, frames_dev, g_heads, p_rows, head_size = far[0].shape
    n_tm = len(ks) + GROUPS
    me = lax.axis_index("tm")
    slots = [(me ^ k, ref) for k, ref in zip(ks, far)]
    slots += [(me // GROUPS * GROUPS + j, near.at[j]) for j in range(GROUPS)]
    frames = n_tm * frames_dev
    slot_rows = frames_dev * p_rows
    block = probs_ref.shape[-1]
    for a in range(3):
        for h in range(g_heads):
            for slot, ref in slots:
                rows = pl.ds(pl.multiple_of(slot * slot_rows, slot_rows), slot_rows)
                wide[a, h, rows] = (
                    ref[a, :, h].reshape(slot_rows, head_size).astype(jnp.float32)
                )
        by_position(wide.at[a], by_pos[a], frames, p_rows)
    row = lax.broadcasted_iota(jnp.int32, (1, block, block), 1) // frames
    col = lax.broadcasted_iota(jnp.int32, (1, block, block), 2) // frames
    scores = blocks_dot(by_pos[0][...], by_pos[1][...], 2, 2) * head_size ** (-0.5)
    scores = jnp.where(row == col, scores, -jnp.inf)
    expo = jnp.exp(scores - jnp.max(scores, axis=-1, keepdims=True))
    probs_ref[...] = expo / jnp.sum(expo, axis=-1, keepdims=True)


def grads_kernel(n_tm, slots, *refs):
    gin = refs[:n_tm]
    q_ref, k_ref, v_ref, probs_ref = refs[n_tm : n_tm + 4]
    outs = refs[n_tm + 4 : 2 * n_tm + 4]
    wide, g_ref, back = refs[2 * n_tm + 4 :]
    g_heads, frames_dev, p_rows, head_size = gin[0].shape
    frames = n_tm * frames_dev
    slot_rows = frames_dev * p_rows
    scale = head_size ** (-0.5)
    me, half = lax.axis_index("tm"), lax.axis_index("fsdp") // 2
    for j, r in enumerate(ROUNDS):
        slot = 2 * ((me // 2) ^ (r // 2)) + (half ^ (r % 2))
        rows = pl.ds(pl.multiple_of(slot * slot_rows, slot_rows), slot_rows)
        for h in range(g_heads):
            wide[h, rows] = gin[j][h].reshape(slot_rows, head_size).astype(jnp.float32)
    by_position(wide, g_ref, frames, p_rows)
    g, probs = g_ref[...], probs_ref[...]
    probs_b = probs.astype(jnp.bfloat16)
    dprobs = blocks_dot(g, v_ref[...], 2, 2)
    row_delta = jnp.sum(probs_b.astype(jnp.float32) * dprobs, axis=-1, keepdims=True)
    dscores = (probs * (dprobs - row_delta)).astype(jnp.bfloat16)
    grads = (
        blocks_dot(dscores, k_ref[...], 2, 1) * scale,
        blocks_dot(dscores, q_ref[...], 1, 1) * scale,
        blocks_dot(probs_b, g, 1, 1),
    )
    per = g.shape[1] // frames
    groups = p_rows // per
    for a, grad in enumerate(grads):
        for h in range(g_heads):
            for p in range(p_rows):
                back[a, h, pl.ds(p, frames, stride=p_rows), :] = grad[
                    h * groups + p // per, p % per * frames : (p % per + 1) * frames
                ]
    for a in range(3):
        for h in range(g_heads):
            for k, out in zip(slots, outs):
                rows = pl.ds(pl.multiple_of((me ^ k) * slot_rows, slot_rows), slot_rows)
                out[a, :, h] = (
                    back[a, h, rows]
                    .astype(jnp.bfloat16)
                    .reshape(frames_dev, p_rows, head_size)
                )


def probs_of(far, near, ks):
    _, frames_dev, g_heads, p_rows, head_size = far[0].shape
    frames = (len(ks) + GROUPS) * frames_dev
    per = max(1, 128 // frames)
    block = per * frames
    count = g_heads * p_rows // per
    return pl.pallas_call(
        functools.partial(probs_kernel, ks),
        out_shape=[jax.ShapeDtypeStruct((count, block, head_size), jnp.bfloat16)] * 3
        + [jax.ShapeDtypeStruct((count, block, block), jnp.float32)],
        in_specs=[VMEM] * (len(ks) + 1),
        out_specs=[VMEM] * 4,
        scratch_shapes=[pltpu.VMEM((3, g_heads, frames * p_rows, head_size), jnp.float32)],
        compiler_params=pltpu.CompilerParams(vmem_limit_bytes=16 * MIB),
        name="probs",
    )(*far, near)


def grads_of(gin, by_pos, slots, shape):
    n_tm = len(gin)
    _, frames_dev, g_heads, p_rows, head_size = shape
    frames = n_tm * frames_dev
    return pl.pallas_call(
        functools.partial(grads_kernel, n_tm, slots),
        out_shape=[jax.ShapeDtypeStruct(shape, jnp.bfloat16)] * n_tm,
        in_specs=[VMEM] * (n_tm + 4),
        out_specs=[VMEM] * n_tm,
        scratch_shapes=[
            pltpu.VMEM((g_heads, frames * p_rows, head_size), jnp.float32),
            pltpu.VMEM(by_pos[0].shape, jnp.bfloat16),
            pltpu.VMEM((3, g_heads, frames * p_rows, head_size), jnp.float32),
        ],
        compiler_params=pltpu.CompilerParams(vmem_limit_bytes=16 * MIB),
        name="grads",
    )(*gin, *by_pos)


def after(later, earlier):
    return lax.optimization_barrier((later, earlier))


def body_permutes(n_tm, n_fsdp, queries, key_states, value_states, out_grad, out_proj):
    _, pos_dev, _, head_size = queries.shape
    p_rows = pos_dev * GROUPS // n_tm
    slots = SLOTS

    def swap(x, bit):
        return lax.ppermute(x, "fsdp", [(i, i ^ bit) for i in range(n_fsdp)])

    def send(message, k):
        return lax.ppermute(message, "tm", [(i, i ^ k) for i in range(n_tm)]) if k else message

    def round_of(message, r):
        kz, kx = r // 2, r % 2
        pairs = []
        for tm in range(n_tm):
            for fs in range(n_fsdp):
                z, y, x, core = tm // 2, tm % 2, fs // 2, fs % 2
                there = (2 * (z ^ kz) + x) * n_fsdp + 2 * (y ^ kx) + core
                pairs.append((tm * n_fsdp + fs, there))
        return lax.ppermute(message, ("tm", "fsdp"), pairs)

    other = swap(out_grad, 2)
    w_other = swap(out_proj, 1)
    heads_out = lambda x: jnp.transpose(x, (0, 2, 1, 3))
    q_k_v = (heads_out(queries), heads_out(key_states), heads_out(value_states))
    far = FAR
    far_messages = list(pack_far(q_k_v, far, p_rows))
    near_message = pack_near(q_k_v, p_rows)
    far_messages[3], w_other = after(far_messages[3], w_other)
    far_qkv = [send(m, k) for m, k in zip(far_messages, far)]
    near_qkv = lax.all_to_all(
        near_message,
        "tm",
        split_axis=0,
        concat_axis=0,
        axis_index_groups=[[b + j for j in range(GROUPS)] for b in range(0, n_tm, GROUPS)],
        tiled=True,
    )
    res_own, w_both = project_own(out_grad, out_proj, w_other, head_size)
    messages = project_other(other, w_both, res_own, n_tm, p_rows)
    gin = [round_of(m, r) for r, m in zip(ROUNDS, messages)]
    grads = grads_of(gin, probs_of(far_qkv, near_qkv, far), slots, far_qkv[0].shape)
    grads = [send(g, k) for g, k in zip(grads, slots)]
    grads = dict(zip(slots, grads))
    early = tuple(k for k in slots if k not in LATE)
    outs = unpack([grads[k] for k in early], early, pos_dev)
    outs = unpack([grads[k] for k in LATE], LATE, pos_dev, outs)
    return tuple(heads_out(g) for g in outs)


def solution(mesh):
    n_tm, n_fsdp = mesh.shape["tm"], mesh.shape["fsdp"]

    def body(queries, key_states, value_states, out_grad, out_proj):
        _, pos_dev, heads, head_size = queries.shape
        fits = (
            n_tm == 2 * GROUPS
            and n_fsdp == GROUPS
            and heads % GROUPS == 0
            and out_proj.shape[0] * GROUPS == heads * head_size
            and pos_dev % 32 == 0
            and head_size == 128
        )
        if fits:
            return body_permutes(
                n_tm, n_fsdp, queries, key_states, value_states, out_grad, out_proj
            )
        return body_any(queries, key_states, value_states, out_grad, out_proj)

    return jax.shard_map(
        body,
        mesh=mesh,
        in_specs=(
            P("tm", "fsdp", None, None),
            P("tm", "fsdp", None, None),
            P("tm", "fsdp", None, None),
            P("tm", "fsdp", None),
            P("fsdp", None),
        ),
        out_specs=(
            P("tm", "fsdp", None, None),
            P("tm", "fsdp", None, None),
            P("tm", "fsdp", None, None),
        ),
        check_vma=False,
    )
```

```python
import functools

import jax
import jax.numpy as jnp
from jax import lax
from jax.experimental import pallas as pl
from jax.experimental.pallas import tpu as pltpu
from jax.sharding import PartitionSpec as P

ANY = pl.BlockSpec(memory_space=pl.ANY)
HBM = pl.BlockSpec(memory_space=pltpu.HBM)
VMEM = pl.BlockSpec(memory_space=pltpu.VMEM)
MIB = 1024 * 1024
SLOTS = (6, 7, 4, 5, 3, 2, 1, 0)
LATE = (5, 4)
FAR = (7, 6, 4, 5)
ROUNDS = (0, 1, 6, 7, 4, 5, 2, 3)
GROUPS = 4


NT = (((1,), (1,)), ((), ()))
dot = functools.partial(lax.dot_general, preferred_element_type=jnp.float32)


def blocks_dot(a, b, over_a, over_b):
    return dot(a, b, (((over_a,), (over_b,)), ((0,), (0,))))


def attend_back(query_block, key_block, value_block, grad_block):
    score_scale = query_block.shape[-1] ** (-0.5)
    scores = (
        jnp.einsum("fphd,gphd->phfg", query_block, key_block, preferred_element_type=jnp.float32)
        * score_scale
    )
    peak = jnp.max(scores, axis=-1, keepdims=True)
    expo = jnp.exp(scores - peak)
    probs = expo / jnp.sum(expo, axis=-1, keepdims=True)
    probs_b = probs.astype(jnp.bfloat16)
    attn_out = jnp.einsum(
        "phfg,gphd->fphd", probs_b, value_block, preferred_element_type=jnp.float32
    )
    row_delta = jnp.einsum("fphd,fphd->phf", grad_block.astype(jnp.float32), attn_out)
    dprobs = jnp.einsum(
        "fphd,gphd->phfg", grad_block, value_block, preferred_element_type=jnp.float32
    )
    dscores = (probs * (dprobs - row_delta[..., None])).astype(jnp.bfloat16)
    query_grad = (
        jnp.einsum("phfg,gphd->fphd", dscores, key_block, preferred_element_type=jnp.float32)
        * score_scale
    ).astype(jnp.bfloat16)
    key_grad = (
        jnp.einsum("phfg,fphd->gphd", dscores, query_block, preferred_element_type=jnp.float32)
        * score_scale
    ).astype(jnp.bfloat16)
    value_grad = jnp.einsum(
        "phfg,fphd->gphd", probs_b, grad_block, preferred_element_type=jnp.float32
    ).astype(jnp.bfloat16)
    return (query_grad, key_grad, value_grad)


def body_any(queries, key_states, value_states, out_grad, out_proj):
    frames_dev, pos_dev, heads, head_size = queries.shape
    flat = out_grad.reshape(frames_dev * pos_dev, out_grad.shape[-1])
    grad_attn = (
        lax.dot_general(
            flat,
            lax.all_gather(out_proj, "fsdp", axis=0, tiled=True),
            (((1,), (1,)), ((), ())),
            preferred_element_type=jnp.float32,
        )
        .astype(jnp.bfloat16)
        .reshape(frames_dev, pos_dev, heads, head_size)
    )
    there = functools.partial(
        lax.all_to_all, axis_name="tm", split_axis=1, concat_axis=0, tiled=True
    )
    back = functools.partial(
        lax.all_to_all, axis_name="tm", split_axis=0, concat_axis=1, tiled=True
    )
    grads = attend_back(there(queries), there(key_states), there(value_states), there(grad_attn))
    return tuple(back(g) for g in grads)


def group_of(tm):
    return 2 * (tm % 2) + tm // 2 % 2


def part_of(tm):
    return tm // GROUPS


def copy_all(copies):
    for copy in copies:
        copy.start()
    for copy in copies:
        copy.wait()


def pack_copies(there, q_k_v, message, sems):
    _, _, g_heads, p_rows, _ = message.shape
    heads = pl.ds(group_of(there) * g_heads, g_heads)
    rows = pl.ds(pl.multiple_of(part_of(there) * p_rows, p_rows), p_rows)
    return [
        pltpu.make_async_copy(ref.at[:, heads, rows], message.at[a], sems.at[a])
        for a, ref in enumerate(q_k_v)
    ]


def pack_far_kernel(ks, *refs):
    q_k_v, outs, (stage, in_sems, out_sems) = refs[:3], refs[3:-3], refs[-3:]
    me = lax.axis_index("tm")
    arrivals = [
        pack_copies(me ^ k, q_k_v, stage.at[j], in_sems.at[j]) for j, k in enumerate(ks)
    ]
    departures = [
        pltpu.make_async_copy(stage.at[j], out, out_sems.at[j]) for j, out in enumerate(outs)
    ]
    for copies in arrivals:
        for copy in copies:
            copy.start()
    for copies, departure in zip(arrivals, departures):
        for copy in copies:
            copy.wait()
        departure.start()
    for departure in departures:
        departure.wait()


def pack_near_kernel(*refs):
    q_k_v, out, stage, sems = refs[:3], refs[3], refs[4], refs[5]
    first = lax.axis_index("tm") // GROUPS * GROUPS
    copy_all(
        [
            copy
            for j in range(GROUPS)
            for copy in pack_copies(first + j, q_k_v, stage.at[j], sems.at[j])
        ]
    )
    out[...] = stage[...]


def message_shape(q, p_rows):
    frames_dev, heads, _, head_size = q.shape
    return (3, frames_dev, heads // GROUPS, p_rows, head_size)


def pack_far(q_k_v, ks, p_rows):
    shape = message_shape(q_k_v[0], p_rows)
    return pl.pallas_call(
        functools.partial(pack_far_kernel, ks),
        out_shape=[jax.ShapeDtypeStruct(shape, q_k_v[0].dtype)] * len(ks),
        in_specs=[HBM] * 3,
        out_specs=[ANY] * len(ks),
        scratch_shapes=[
            pltpu.VMEM((len(ks),) + shape, q_k_v[0].dtype),
            pltpu.SemaphoreType.DMA((len(ks), 3)),
            pltpu.SemaphoreType.DMA((len(ks),)),
        ],
        compiler_params=pltpu.CompilerParams(vmem_limit_bytes=4 * MIB),
        name="pack_far",
    )(*(pltpu.with_memory_space_constraint(x, pltpu.HBM) for x in q_k_v))


def pack_near(q_k_v, p_rows):
    shape = (GROUPS,) + message_shape(q_k_v[0], p_rows)
    return pl.pallas_call(
        pack_near_kernel,
        out_shape=jax.ShapeDtypeStruct(shape, q_k_v[0].dtype),
        in_specs=[HBM] * 3,
        out_specs=VMEM,
        scratch_shapes=[
            pltpu.VMEM(shape, q_k_v[0].dtype),
            pltpu.SemaphoreType.DMA((GROUPS, 3)),
        ],
        compiler_params=pltpu.CompilerParams(vmem_limit_bytes=4 * MIB),
        name="pack_near",
    )(*(pltpu.with_memory_space_constraint(x, pltpu.HBM) for x in q_k_v))


def unpack_kernel(ks, *refs):
    grads, outs, sems = refs[: len(ks)], refs[-4:-1], refs[-1]
    me = lax.axis_index("tm")
    _, _, g_heads, p_rows, _ = grads[0].shape
    copies = []
    for j, k in enumerate(ks):
        there = me ^ k
        heads = pl.ds(group_of(there) * g_heads, g_heads)
        rows = pl.ds(pl.multiple_of(part_of(there) * p_rows, p_rows), p_rows)
        for a, ref in enumerate(outs):
            copies.append(
                pltpu.make_async_copy(grads[j].at[a], ref.at[:, heads, rows], sems.at[j, a])
            )
    copy_all(copies)


def unpack(grads, ks, pos_dev, before=()):
    _, frames_dev, g_heads, _, head_size = grads[0].shape
    shape = (frames_dev, g_heads * GROUPS, pos_dev, head_size)
    n = len(ks)
    return pl.pallas_call(
        functools.partial(unpack_kernel, ks),
        out_shape=[jax.ShapeDtypeStruct(shape, grads[0].dtype)] * 3,
        in_specs=[ANY] * n + [HBM] * len(before),
        out_specs=[HBM] * 3,
        scratch_shapes=[pltpu.SemaphoreType.DMA((n, 3))],
        input_output_aliases={n + a: a for a in range(len(before))},
        compiler_params=pltpu.CompilerParams(vmem_limit_bytes=1 * MIB),
        name="unpack",
    )(*grads, *before)


def project_into(res, at, w, out):
    g_heads, frames_dev, pos_dev, head_size = res.shape[2:]
    for h in range(g_heads):
        res[w, at, h] = out[:, h * head_size : (h + 1) * head_size].reshape(
            frames_dev, pos_dev, head_size
        )


def flat(rows_ref):
    frames_dev, pos_dev, width = rows_ref.shape
    return rows_ref[...].reshape(frames_dev * pos_dev, width)


def project_own_kernel(own_ref, w_own_ref, w_other_ref, res, w_ref, rows_ref, sems):
    core = lax.rem(lax.axis_index("fsdp"), 2)
    w_copies = [
        pltpu.make_async_copy(ref, w_ref.at[i], sems.at[i])
        for i, ref in enumerate((w_own_ref, w_other_ref))
    ]
    rows_copy = pltpu.make_async_copy(own_ref, rows_ref, sems.at[2])
    for copy in (w_copies[0], rows_copy, w_copies[1]):
        copy.start()
    rows_copy.wait()
    rows = flat(rows_ref)
    for i, copy in enumerate(w_copies):
        copy.wait()
        project_into(res, 0, core ^ i, dot(rows, w_ref[i], NT).astype(jnp.bfloat16))


def project_other_kernel(n_tm, other_ref, w_ref, own_ref, *refs):
    outs, res, sems = refs[:n_tm], refs[n_tm], refs[n_tm + 1]
    me, fs = lax.axis_index("tm"), lax.axis_index("fsdp")
    half, core = fs // 2, lax.rem(fs, 2)
    p_rows = outs[0].shape[2]
    y, z = lax.rem(me, 2), me // 2
    own, other = [], []
    for j, r in enumerate(ROUNDS):
        there_z = z ^ (r // 2)
        part = pl.ds(pl.multiple_of((there_z // 2) * p_rows, p_rows), p_rows)
        at = lax.rem(there_z, 2)
        own.append(
            pltpu.make_async_copy(own_ref.at[at, 0, :, :, part], outs[j], sems.at[j])
        )
        other.append(pltpu.make_async_copy(res.at[at, :, :, part], outs[j], sems.at[j]))
    mine = [half == y ^ (r % 2) for r in ROUNDS]
    for copy, here in zip(own, mine):
        pl.when(here)(copy.start)
    rows = flat(other_ref)
    for i in range(2):
        out = dot(rows, w_ref[i], NT).astype(jnp.bfloat16)
        g_heads, frames_dev, pos_dev, head_size = res.shape[1:]
        for h in range(g_heads):
            res[core ^ i, h] = out[:, h * head_size : (h + 1) * head_size].reshape(
                frames_dev, pos_dev, head_size
            )
    for copy, here in zip(other, mine):
        pl.when(jnp.logical_not(here))(copy.start)
    for copy in other:
        copy.wait()


def project_cost(own, w_own, weight):
    rows = own.shape[0] * own.shape[1]
    return pl.CostEstimate(
        flops=weight * 4 * rows * w_own.shape[0] * own.shape[2],
        bytes_accessed=2 * own.shape[2] * (rows + 2 * w_own.shape[0]),
        transcendentals=0,
    )


def project_own(own, w_own, w_other, head_size):
    frames_dev, pos_dev, width = own.shape
    w_rows = w_own.shape[0]
    return pl.pallas_call(
        project_own_kernel,
        out_shape=[
            jax.ShapeDtypeStruct(
                (2, 1, w_rows // head_size, frames_dev, pos_dev, head_size), own.dtype
            ),
            jax.ShapeDtypeStruct((2, w_rows, width), own.dtype),
        ],
        in_specs=[HBM] * 3,
        out_specs=[VMEM] * 2,
        scratch_shapes=[
            pltpu.VMEM(own.shape, own.dtype),
            pltpu.SemaphoreType.DMA((3,)),
        ],
        compiler_params=pltpu.CompilerParams(vmem_limit_bytes=14 * MIB),
        cost_estimate=project_cost(own, w_own, 1),
        name="project_own",
    )(*(pltpu.with_memory_space_constraint(x, pltpu.HBM) for x in (own, w_own, w_other)))


def project_other(other, w, res_own, n_tm, p_rows):
    _, _, g_heads, frames_dev, pos_dev, head_size = res_own.shape
    shape = (g_heads, frames_dev, p_rows, head_size)
    return pl.pallas_call(
        functools.partial(project_other_kernel, n_tm),
        out_shape=[jax.ShapeDtypeStruct(shape, other.dtype)] * n_tm,
        in_specs=[VMEM] * 3,
        out_specs=[ANY] * n_tm,
        scratch_shapes=[
            pltpu.VMEM((2,) + res_own.shape[2:], jnp.bfloat16),
            pltpu.SemaphoreType.DMA((n_tm,)),
        ],
        compiler_params=pltpu.CompilerParams(vmem_limit_bytes=14 * MIB),
        cost_estimate=project_cost(other, w[0], 16),
        name="project_other",
    )(other, w, res_own)


def by_position(wide, out, frames, p_rows):
    per = out.shape[1] // frames
    groups = p_rows // per
    for h in range(wide.shape[0]):
        for p in range(p_rows):
            rows = slice(p % per * frames, (p % per + 1) * frames)
            out[h * groups + p // per, rows] = wide[h, pl.ds(p, frames, stride=p_rows), :].astype(
                jnp.bfloat16
            )


def probs_kernel(ks, *refs):
    far, near = refs[: len(ks)], refs[len(ks)]
    by_pos, probs_ref, wide = refs[len(ks) + 1 : len(ks) + 4], refs[len(ks) + 4], refs[-1]
    _, frames_dev, g_heads, p_rows, head_size = far[0].shape
    n_tm = len(ks) + GROUPS
    me = lax.axis_index("tm")
    slots = [(me ^ k, ref) for k, ref in zip(ks, far)]
    slots += [(me // GROUPS * GROUPS + j, near.at[j]) for j in range(GROUPS)]
    frames = n_tm * frames_dev
    slot_rows = frames_dev * p_rows
    block = probs_ref.shape[-1]
    for a in range(3):
        for h in range(g_heads):
            for slot, ref in slots:
                rows = pl.ds(pl.multiple_of(slot * slot_rows, slot_rows), slot_rows)
                wide[a, h, rows] = (
                    ref[a, :, h].reshape(slot_rows, head_size).astype(jnp.float32)
                )
        by_position(wide.at[a], by_pos[a], frames, p_rows)
    row = lax.broadcasted_iota(jnp.int32, (1, block, block), 1) // frames
    col = lax.broadcasted_iota(jnp.int32, (1, block, block), 2) // frames
    scores = blocks_dot(by_pos[0][...], by_pos[1][...], 2, 2) * head_size ** (-0.5)
    scores = jnp.where(row == col, scores, -jnp.inf)
    expo = jnp.exp(scores - jnp.max(scores, axis=-1, keepdims=True))
    probs_ref[...] = expo / jnp.sum(expo, axis=-1, keepdims=True)


def grads_kernel(n_tm, slots, *refs):
    gin = refs[:n_tm]
    q_ref, k_ref, v_ref, probs_ref = refs[n_tm : n_tm + 4]
    outs = refs[n_tm + 4 : 2 * n_tm + 4]
    wide, g_ref, back = refs[2 * n_tm + 4 :]
    g_heads, frames_dev, p_rows, head_size = gin[0].shape
    frames = n_tm * frames_dev
    slot_rows = frames_dev * p_rows
    scale = head_size ** (-0.5)
    me, half = lax.axis_index("tm"), lax.axis_index("fsdp") // 2
    for j, r in enumerate(ROUNDS):
        slot = 2 * ((me // 2) ^ (r // 2)) + (half ^ (r % 2))
        rows = pl.ds(pl.multiple_of(slot * slot_rows, slot_rows), slot_rows)
        for h in range(g_heads):
            wide[h, rows] = gin[j][h].reshape(slot_rows, head_size).astype(jnp.float32)
    by_position(wide, g_ref, frames, p_rows)
    g, probs = g_ref[...], probs_ref[...]
    probs_b = probs.astype(jnp.bfloat16)
    dprobs = blocks_dot(g, v_ref[...], 2, 2)
    row_delta = jnp.sum(probs_b.astype(jnp.float32) * dprobs, axis=-1, keepdims=True)
    dscores = (probs * (dprobs - row_delta)).astype(jnp.bfloat16)
    grads = (
        blocks_dot(dscores, k_ref[...], 2, 1) * scale,
        blocks_dot(dscores, q_ref[...], 1, 1) * scale,
        blocks_dot(probs_b, g, 1, 1),
    )
    per = g.shape[1] // frames
    groups = p_rows // per
    for a, grad in enumerate(grads):
        for h in range(g_heads):
            for p in range(p_rows):
                back[a, h, pl.ds(p, frames, stride=p_rows), :] = grad[
                    h * groups + p // per, p % per * frames : (p % per + 1) * frames
                ]
    for a in range(3):
        for h in range(g_heads):
            for k, out in zip(slots, outs):
                rows = pl.ds(pl.multiple_of((me ^ k) * slot_rows, slot_rows), slot_rows)
                out[a, :, h] = (
                    back[a, h, rows]
                    .astype(jnp.bfloat16)
                    .reshape(frames_dev, p_rows, head_size)
                )


def probs_of(far, near, ks):
    _, frames_dev, g_heads, p_rows, head_size = far[0].shape
    frames = (len(ks) + GROUPS) * frames_dev
    per = max(1, 128 // frames)
    block = per * frames
    count = g_heads * p_rows // per
    return pl.pallas_call(
        functools.partial(probs_kernel, ks),
        out_shape=[jax.ShapeDtypeStruct((count, block, head_size), jnp.bfloat16)] * 3
        + [jax.ShapeDtypeStruct((count, block, block), jnp.float32)],
        in_specs=[VMEM] * (len(ks) + 1),
        out_specs=[VMEM] * 4,
        scratch_shapes=[pltpu.VMEM((3, g_heads, frames * p_rows, head_size), jnp.float32)],
        compiler_params=pltpu.CompilerParams(vmem_limit_bytes=16 * MIB),
        name="probs",
    )(*far, near)


def grads_of(gin, by_pos, slots, shape):
    n_tm = len(gin)
    _, frames_dev, g_heads, p_rows, head_size = shape
    frames = n_tm * frames_dev
    return pl.pallas_call(
        functools.partial(grads_kernel, n_tm, slots),
        out_shape=[jax.ShapeDtypeStruct(shape, jnp.bfloat16)] * n_tm,
        in_specs=[VMEM] * (n_tm + 4),
        out_specs=[VMEM] * n_tm,
        scratch_shapes=[
            pltpu.VMEM((g_heads, frames * p_rows, head_size), jnp.float32),
            pltpu.VMEM(by_pos[0].shape, jnp.bfloat16),
            pltpu.VMEM((3, g_heads, frames * p_rows, head_size), jnp.float32),
        ],
        compiler_params=pltpu.CompilerParams(vmem_limit_bytes=16 * MIB),
        name="grads",
    )(*gin, *by_pos)


def after(later, earlier):
    return lax.optimization_barrier((later, earlier))


def body_permutes(n_tm, n_fsdp, queries, key_states, value_states, out_grad, out_proj):
    _, pos_dev, _, head_size = queries.shape
    p_rows = pos_dev * GROUPS // n_tm
    slots = SLOTS

    def swap(x, bit):
        return lax.ppermute(x, "fsdp", [(i, i ^ bit) for i in range(n_fsdp)])

    def send(message, k):
        return lax.ppermute(message, "tm", [(i, i ^ k) for i in range(n_tm)]) if k else message

    def round_of(message, r):
        kz, kx = r // 2, r % 2
        pairs = []
        for tm in range(n_tm):
            for fs in range(n_fsdp):
                z, y, x, core = tm // 2, tm % 2, fs // 2, fs % 2
                there = (2 * (z ^ kz) + x) * n_fsdp + 2 * (y ^ kx) + core
                pairs.append((tm * n_fsdp + fs, there))
        return lax.ppermute(message, ("tm", "fsdp"), pairs)

    other = swap(out_grad, 2)
    w_other = swap(out_proj, 1)
    heads_out = lambda x: jnp.transpose(x, (0, 2, 1, 3))
    q_k_v = (heads_out(queries), heads_out(key_states), heads_out(value_states))
    far = FAR
    far_messages = list(pack_far(q_k_v, far, p_rows))
    near_message = pack_near(q_k_v, p_rows)
    far_messages[3], w_other = after(far_messages[3], w_other)
    far_qkv = [send(m, k) for m, k in zip(far_messages, far)]
    near_qkv = lax.all_to_all(
        near_message,
        "tm",
        split_axis=0,
        concat_axis=0,
        axis_index_groups=[[b + j for j in range(GROUPS)] for b in range(0, n_tm, GROUPS)],
        tiled=True,
    )
    res_own, w_both = project_own(out_grad, out_proj, w_other, head_size)
    messages = project_other(other, w_both, res_own, n_tm, p_rows)
    gin = [round_of(m, r) for r, m in zip(ROUNDS, messages)]
    grads = grads_of(gin, probs_of(far_qkv, near_qkv, far), slots, far_qkv[0].shape)
    grads = [send(g, k) for g, k in zip(grads, slots)]
    grads = dict(zip(slots, grads))
    early = tuple(k for k in slots if k not in LATE)
    outs = unpack([grads[k] for k in early], early, pos_dev)
    outs = unpack([grads[k] for k in LATE], LATE, pos_dev, outs)
    return tuple(heads_out(g) for g in outs)


def solution(mesh):
    n_tm, n_fsdp = mesh.shape["tm"], mesh.shape["fsdp"]

    def body(queries, key_states, value_states, out_grad, out_proj):
        _, pos_dev, heads, head_size = queries.shape
        fits = (
            n_tm == 2 * GROUPS
            and n_fsdp == GROUPS
            and heads % GROUPS == 0
            and out_proj.shape[0] * GROUPS == heads * head_size
            and pos_dev % 32 == 0
            and head_size == 128
        )
        if fits:
            return body_permutes(
                n_tm, n_fsdp, queries, key_states, value_states, out_grad, out_proj
            )
        return body_any(queries, key_states, value_states, out_grad, out_proj)

    return jax.shard_map(
        body,
        mesh=mesh,
        in_specs=(
            P("tm", "fsdp", None, None),
            P("tm", "fsdp", None, None),
            P("tm", "fsdp", None, None),
            P("tm", "fsdp", None),
            P("fsdp", None),
        ),
        out_specs=(
            P("tm", "fsdp", None, None),
            P("tm", "fsdp", None, None),
            P("tm", "fsdp", None, None),
        ),
        check_vma=False,
    )
```
